128 devices in a mesh: rep: 2 (over y_lo), tx: 8 (over x, y_hi), ty: 8 (over z, core).
Axes of the slice: x: 4, y: 4 (y_hi: 2, y_lo: 2; y = y_hi * 2 + y_lo), z: 4, core: 2. Of those that a mesh axis runs over, the one named last changes fastest.
Arguments:
- density: bfloat16 [2, 256, 512, 128], P('rep', 'tx', 'ty'), may hold values from -6 to 6
- kernel_one: bfloat16 [16, 4, 3, 3, 3], replicated, may hold values from -0.625 to 0.625
- kernel_two: bfloat16 [16, 16, 3, 3, 3], replicated, may hold values from -0.3125 to 0.3125
- cotangent: bfloat16 [2, 128, 256, 256], P('rep', 'tx', 'ty'), may hold values from -30 to 30
Outputs:
- features: bfloat16 [2, 128, 256, 256], P('rep', 'tx', 'ty')
- grad_one: float32 [16, 4, 3, 3, 3], replicated
- grad_two: float32 [16, 16, 3, 3, 3], replicated
The draws below stay inside these ranges and needn't reach their ends.
All inputs are finite; a program needn't handle non-finite values.
Results may differ from the reference program's by a relative error of at most 0.015.
Values may be sent and summed in bfloat16 or wider, within the bound.
No kernel may reach another device: no remote copies, remote signals or barrier semaphores. Data moves between devices by JAX's collectives and lax.ppermute only.
A program may use at most 320 MiB of HBM per device.

```python
import jax
import jax.numpy as jnp
from jax import lax

CIN = 4
CH = 16
SAMPLES = 1
DEPTH = 32
NX = 256
NY = 512
BATCH = 2
N_REP = 2


def draw_cotangent(key, part):
    shape = (SAMPLES * N_REP, NX // 2, NY // 2, CH * (DEPTH // 2))
    half_x = NX // 2
    ramp = 1.0 + 2.0 * jnp.arange(half_x, dtype=jnp.float32) / max(half_x - 1, 1)
    ramp = ramp.reshape(1, half_x, 1, 1)
    base = jax.random.normal(key, shape, jnp.float32)
    values = jnp.clip(base, -6.0, 6.0) * ramp
    return values.astype(jnp.bfloat16)


def block_scale(stream_key, shape, cuts, least, top_value):
    gain, own = 1.0, jax.random.fold_in(stream_key, 6)
    for axis_at, blocks in cuts:
        steps = jnp.exp(jax.random.uniform(jax.random.fold_in(own, axis_at), (blocks,), jnp.float32, least / len(cuts), top_value / len(cuts)))
        gain = gain * jnp.repeat(steps, shape[axis_at] // blocks).reshape([-1 if axis == axis_at else 1 for axis in range(len(shape))])
    return gain


def scatter_about(own_key, shape, deviation, limit, split=(), kind=jnp.bfloat16):
    values = jax.random.normal(own_key, shape, jnp.float32) * deviation
    if len(split) > 0:
        values = block_scale(own_key, shape, split, -0.22, 0.18) * values
    return jnp.clip(values, min=-limit, max=limit).astype(kind)


def setup_inputs(seed: int = 0) -> dict:
    seeds = jax.random.split(jax.random.key(seed), 5)
    return {
        "density": scatter_about(seeds[0], (BATCH, NX, NY, CIN * DEPTH), 1.0, 6.0, ((0, 2), (1, 8), (2, 8))),
        "kernel_one": scatter_about(seeds[1], (CH, CIN, 3, 3, 3), (CIN * 27) ** -0.5, 0.625),
        "kernel_two": scatter_about(seeds[2], (CH, CH, 3, 3, 3), (CH * 27) ** -0.5, 0.3125),
        "cotangent": draw_cotangent(jax.random.fold_in(seeds[4], 71), 0),
    }


leak_slope = 0.3


def convolve(lhs, rhs, specs):
    return lax.conv_general_dilated(lhs.astype(jnp.float32), rhs.astype(jnp.float32), (1, 1, 1), "VALID", dimension_numbers=specs, precision=lax.Precision.HIGHEST, preferred_element_type=jnp.float32)


def border(field):
    wrapped = jnp.pad(field, ((0, 0), (0, 0), (0, 0), (1, 1), (1, 1)), mode="wrap")
    return jnp.pad(wrapped, ((0, 0), (0, 0), (1, 1), (0, 0), (0, 0)))


def pooling(field):
    s, c, d, x, y = field.shape
    blocks = field.astype(jnp.float32).reshape(s, c, d // 2, 2, x // 2, 2, y // 2, 2)
    return jnp.mean(blocks, axis=(3, 5, 7))


def upsample(field):
    s, c, d, x, y = field.shape
    grown = jnp.broadcast_to(field[:, :, :, None, :, None, :, None], (s, c, d, 2, x, 2, y, 2))
    return grown.reshape(s, c, 2 * d, 2 * x, 2 * y)


def unpack(field, channels):
    s, x, y, merged = field.shape
    return jnp.transpose(field.reshape(s, x, y, channels, merged // channels), (0, 3, 4, 1, 2))


def packing(field):
    s, c, d, x, y = field.shape
    return jnp.transpose(field, (0, 3, 4, 1, 2)).reshape(s, x, y, c * d)


def reference(density, kernel_one, kernel_two, cotangent):
    forward = ("NCDHW", "OIDHW", "NCDHW")
    weight_form = ("CNDHW", "IODHW", "CNDHW")
    backward = ("NCDHW", "IODHW", "NCDHW")
    flipped = kernel_two[:, :, ::-1, ::-1, ::-1]
    fields = unpack(density, CIN)
    grad_fields = unpack(cotangent, CH)

    def one_replica(inputs):
        slab, grads = inputs
        padded = border(slab)
        pre = convolve(padded, kernel_one, forward)
        act = jnp.where(pre > 0, pre, leak_slope * pre).astype(jnp.bfloat16)
        pooled = pooling(act).astype(jnp.bfloat16)
        pooled_pad = border(pooled)
        features = convolve(pooled_pad, kernel_two, forward).astype(jnp.bfloat16)
        slab_two = convolve(pooled_pad, grads, weight_form)
        back_pooled = convolve(border(grads), flipped, backward).astype(jnp.bfloat16)
        slope = jnp.where(pre > 0, 1.0, leak_slope).astype(jnp.float32)
        back_pre = (upsample(back_pooled.astype(jnp.float32)) * 0.125 * slope).astype(jnp.bfloat16)
        slab_one = convolve(padded, back_pre, weight_form)
        return features, slab_one, slab_two

    slabs = fields.reshape((N_REP, SAMPLES) + fields.shape[1:])
    grads = grad_fields.reshape((N_REP, SAMPLES) + grad_fields.shape[1:])
    features, ones, twos = lax.map(one_replica, (slabs, grads))
    features = packing(features.reshape(grad_fields.shape))
    grad_one = jnp.sum(ones, axis=0) / N_REP
    grad_two = jnp.sum(twos, axis=0) / N_REP
    return features, grad_one, grad_two
```

```python
import functools

import jax
import jax.numpy as jnp
from jax import lax
from jax.experimental import pallas as pl
from jax.experimental.pallas import tpu as pltpu
from jax.sharding import PartitionSpec as P

CIN = 4
CH = 16
LEAK = 0.3
F32 = jnp.float32
BF16 = jnp.bfloat16
NXT = 32
NYT = 64
HX = NXT // 2
HY = NYT // 2
DROW = 80
CROW = 48
VMEM_LIMIT = 48 * 1024 * 1024


def dot_nt(lhs, rhs):
    return lax.dot_general(lhs, rhs, (((1,), (1,)), ((), ())), preferred_element_type=F32)


def dot_nn(lhs, rhs):
    return lax.dot_general(lhs, rhs, (((1,), (0,)), ((), ())), preferred_element_type=F32)


def iota(shape, dim):
    return lax.broadcasted_iota(jnp.int32, shape, dim)


def pack_y_kernel(d_ref, c_ref, up_ref, down_ref, ds, cs):
    for out, low, row, crow in ((down_ref, True, 0, 0), (up_ref, False, 13, 15)):
        at, cat = (0, 0) if low else (NYT - 16, HY - 16)
        ds[...] = d_ref[:, at : at + 16, :].astype(F32).reshape(NXT * 16, 128)
        for half in range(2):
            part = c_ref[:, cat : cat + 16, half * 128 : half * 128 + 128]
            cs[half] = part.astype(F32).reshape(HX * 16, 128)
        for k in range(3):
            out[k * 32 : k * 32 + 32, :] = ds[pl.ds(row + k, 32, stride=16), :].astype(BF16)
        for half in range(2):
            edge = cs[half, pl.ds(crow, 16, stride=16), :]
            out[96 + half * 16 : 112 + half * 16, :] = edge.astype(BF16)


def pack_x_kernel(d_ref, c_ref, lo_ref, hi_ref, up_ref, down_ref, ls, hs, ms):
    ls[...] = lo_ref[...].astype(F32)
    hs[...] = hi_ref[...].astype(F32)
    for out, x, cx in ((down_ref, 0, 0), (up_ref, NXT - 3, HX - 1)):
        out[0:192, :] = d_ref[x : x + 3, :, :].reshape(192, 128)
        out[192:224, :] = c_ref[cx, :, 0:128]
        out[224:256, :] = c_ref[cx, :, 128:256]
        for side, src in enumerate((ls, hs)):
            for k in range(3):
                ms[side * 9 + 3 * k : side * 9 + 3 * k + 3, :] = src[k * 32 + x : k * 32 + x + 3, :]
            for half in range(2):
                at = 18 + side * 2 + half
                ms[at : at + 1, :] = src[96 + half * 16 + cx : 97 + half * 16 + cx, :]
        ms[22:32, :] = jnp.zeros((10, 128), F32)
        out[256:288, :] = ms[...].astype(BF16)


def weights_kernel(k1_ref, k2_ref, w1_ref, wb_ref, w2_ref, s1, so, c1, c2):
    for t in range(27):
        s1[4 * t : 4 * t + 4, 0:CH] = k1_ref[t].astype(F32)
    s1[108:128, :] = jnp.zeros((20, 128), F32)
    k1t = s1[...].T[0:CH].astype(BF16)
    so[...] = jnp.zeros(so.shape, F32)
    for t in range(27):
        g, j = t // 8, t % 8
        so[g * 32 : g * 32 + 16, j * 16 : j * 16 + 16] = k2_ref[t].astype(F32)
    for g in range(4):
        for j in range(8):
            if g * 8 + j < 27:
                s1[j * 16 : j * 16 + 16, 0:CH] = k2_ref[g * 8 + j].astype(F32)
        so[g * 32 + 16 : g * 32 + 32, :] = s1[...].T[0:CH]
    rep1 = (iota((128, 27 * 128), 0) == iota((128, 27 * 128), 1) // 32).astype(BF16)
    c1[...] = dot_nn(k1t, rep1)
    rep2 = (iota((128, 2048), 0) == iota((128, 2048), 1) // 16).astype(BF16)
    c2[...] = dot_nn(so[...].astype(BF16), rep2)

    zero = jnp.zeros((), F32)
    for pd in range(2):
        gap = iota((1, 16, 128), 2) % 32 - 2 * iota((1, 16, 128), 1) - pd
        for kx in range(3):
            for ky in range(3):
                acc = jnp.zeros((16, 16, 128), F32)
                for kd in range(3):
                    t = kd * 9 + kx * 3 + ky
                    row = c1[:, t * 128 : t * 128 + 128][:, None, :]
                    acc = jnp.where(gap == kd - 1, row, acc)
                at = (kx * 3 + ky) * 128
                w1_ref[pd * 256 : pd * 256 + 256, at : at + 128] = acc.reshape(256, 128).astype(BF16)
    gap = iota((1, 16, 256), 2) % 16 - iota((1, 16, 256), 1)
    for kx in range(3):
        for ky in range(3):
            fwd = jnp.zeros((16, 16, 256), F32)
            bwd = jnp.zeros((16, 16, 256), F32)
            for kd in range(3):
                t = kd * 9 + kx * 3 + ky
                g, j = t // 8, t % 8
                row = c2[g * 32 : g * 32 + 16, j * 256 : j * 256 + 256][:, None, :]
                fwd = jnp.where(gap == kd - 1, row, fwd)
                row = c2[g * 32 + 16 : g * 32 + 32, j * 256 : j * 256 + 256][:, None, :]
                bwd = jnp.where(gap == 1 - kd, row, bwd)
            at = (kx * 3 + ky) * 256
            w2_ref[:, at : at + 256] = fwd.reshape(256, 256).astype(BF16)
            at = ((2 - kx) * 3 + 2 - ky) * 256
            wb_ref[:, at : at + 256] = bwd.reshape(256, 256).astype(BF16)


def fill_density(d_ref, lo_ref, hi_ref, xlo_ref, xhi_ref, corner, dp):
    for x in range(NXT):
        dp[(x + 4) * DROW + 8 : (x + 4) * DROW + 8 + NYT, :] = d_ref[x].astype(F32)
    for k in range(3):
        dp[pl.ds(4 * DROW + 5 + k, 32, stride=DROW), :] = lo_ref[k * 32 : k * 32 + 32, :].astype(F32)
        dp[pl.ds(4 * DROW + 8 + NYT + k, 32, stride=DROW), :] = hi_ref[k * 32 : k * 32 + 32, :].astype(F32)
    for base, src, at in ((1, xlo_ref, 0), (4 + NXT, xhi_ref, 32)):
        corner[at : at + 32, :] = src[256:288, :].astype(F32)
        for k in range(3):
            dp[(base + k) * DROW + 8 : (base + k) * DROW + 8 + NYT, :] = src[k * 64 : k * 64 + 64, :].astype(F32)
        for side, y in ((0, 5), (1, 8 + NYT)):
            for ky in range(3):
                for kx in range(3):
                    row = (base + kx) * DROW + y + ky
                    dp[row : row + 1, :] = corner[at + side * 9 + 3 * ky + kx : at + side * 9 + 3 * ky + kx + 1, :]


def fill_cotangent(c_ref, lo_ref, hi_ref, xlo_ref, xhi_ref, corner, cp):
    for half in range(2):
        for x in range(HX):
            at = (x + 1) * CROW + 8
            cp[half, at : at + HY, :] = c_ref[x, :, half * 128 : half * 128 + 128].astype(F32)
        rows = slice(96 + half * 16, 112 + half * 16)
        cp[half, pl.ds(CROW + 7, 16, stride=CROW), :] = lo_ref[rows, :].astype(F32)
        cp[half, pl.ds(CROW + 8 + HY, 16, stride=CROW), :] = hi_ref[rows, :].astype(F32)
        for base, src, at in ((0, xlo_ref, 0), (HX + 1, xhi_ref, 32)):
            cp[half, base * CROW + 8 : base * CROW + 8 + HY, :] = src[192 + half * 32 : 224 + half * 32, :].astype(F32)
            for side, y in ((0, 7), (1, 8 + HY)):
                row = at + 18 + side * 2 + half
                cp[half, base * CROW + y : base * CROW + y + 1, :] = corner[row : row + 1, :]


def fine_taps(dp, taps):
    for x in range(-3, NXT + 3):
        q = x % 2
        at = ((x - q) // 2 + 2) * HY
        for t in range(4):
            rows = dp[pl.ds((x + 4) * DROW + 7 + t, HY, stride=2), :]
            taps[q, at : at + HY, t * 128 : t * 128 + 128] = rows.astype(BF16)


def coarse_taps(padded, taps):
    for x in range(HX + 2):
        for k in range(3):
            for half in range(2):
                rows = padded[half, x * CROW + 7 + k : x * CROW + 7 + k + HY, :]
                lane = k * 256 + half * 128
                taps[x * HY : x * HY + HY, lane : lane + 128] = rows.astype(BF16)


def fine_patch(taps, first, count, px, py):
    parts = []
    for kx in range(3):
        s = px + kx - 1
        q = s % 2
        at = (first + (s - q) // 2 + 2) * HY
        parts.append(taps[q, at : at + count * HY, py * 128 : py * 128 + 384])
    return jnp.concatenate(parts, axis=1)


def coarse_patch(taps, first, count):
    parts = [taps[(first + k) * HY : (first + k + count) * HY, :] for k in range(3)]
    return jnp.concatenate(parts, axis=1)


def leaky_rounded(pre):
    return jnp.where(pre > 0, pre, LEAK * pre).astype(BF16).astype(F32)


def rim_patches(dp, taps, rim):
    for px in range(2):
        for py in range(2):
            at = (px * 2 + py) * 128
            rim[at : at + 32, :] = fine_patch(taps, -1, 1, px, py)
            rim[at + 32 : at + 64, :] = fine_patch(taps, HX, 1, px, py)
            for side, y in ((0, -3), (1, NYT - 1)):
                for kx in range(3):
                    for ky in range(3):
                        start = (1 + px + kx) * DROW + 8 + y + py + ky
                        rows = dp[pl.ds(start, 18, stride=2 * DROW), :]
                        rows = jnp.concatenate([rows, jnp.zeros((14, 128), F32)], axis=0)
                        lane = (kx * 3 + ky) * 128
                        rim[at + 64 + side * 32 : at + 96 + side * 32, lane : lane + 128] = rows.astype(BF16)


def split_dot(select, values):
    high = values.astype(BF16)
    low = (values - high.astype(F32)).astype(BF16)
    return dot_nt(select, high) + dot_nt(select, low)


def extract(g1, g2, out_ref, a1, a2):
    for kd in range(3):
        for m in range(9):
            acc = jnp.zeros((16, 16, 128), F32)
            for pd in range(2):
                gap = iota((1, 16, 128), 2) % 32 - 2 * iota((1, 16, 128), 1) - pd
                part = g1[pd * 256 : pd * 256 + 256, m * 128 : m * 128 + 128].reshape(16, 16, 128)
                acc = acc + jnp.where(gap == kd - 1, part, 0.0)
            a1[(m * 3 + kd) * 16 : (m * 3 + kd) * 16 + 16, :] = jnp.sum(acc, axis=1)
            gap = iota((1, 16, 256), 2) % 16 - iota((1, 16, 256), 1)
            part = g2[:, m * 256 : m * 256 + 256].reshape(16, 16, 256)
            a2[(m * 3 + kd) * 16 : (m * 3 + kd) * 16 + 16, :] = jnp.sum(jnp.where(gap == 1 - kd, part, 0.0), axis=1)
    a1[432:512, :] = jnp.zeros((80, 128), F32)
    a2[432:512, :] = jnp.zeros((80, 256), F32)
    pick2 = (iota((16, 256), 1) // 16 == iota((16, 256), 0)).astype(BF16)
    pick1 = (iota((16, 128), 1) // 32 == iota((16, 128), 0)).astype(BF16)
    out_ref[0:16, :] = split_dot(pick2, a2[...])
    out_ref[16:24, :] = split_dot(pick1, a1[...])[0:8]


def main_kernel(
    d_ref, c_ref, lo_ref, hi_ref, xlo_ref, xhi_ref, w1_ref, wb_ref, w2_ref, feat_ref, grad_ref,
    dp, cp, pp, corner, ft, ct, pt, rim, bpre, g1, g2, a1, a2,
):
    fill_density(d_ref, lo_ref, hi_ref, xlo_ref, xhi_ref, corner, dp)
    fill_cotangent(c_ref, lo_ref, hi_ref, xlo_ref, xhi_ref, corner, cp)
    fine_taps(dp, ft)
    coarse_taps(cp, ct)
    rim_patches(dp, ft, rim)

    total = jnp.zeros((256, 128), F32)
    for c in range(4):
        act = leaky_rounded(dot_nt(w1_ref[...], rim[c * 128 : c * 128 + 128, :]))
        total = total + act[0:256] + act[256:512]
    edge = (total * 0.125).T.astype(BF16).astype(F32)
    for half in range(2):
        lanes = slice(half * 128, half * 128 + 128)
        pp[half, 8:40, :] = edge[0:32, lanes]
        pp[half, (HX + 1) * CROW + 8 : (HX + 1) * CROW + 40, :] = edge[32:64, lanes]
        pp[half, pl.ds(7, 18, stride=CROW), :] = edge[64:82, lanes]
        pp[half, pl.ds(8 + HY, 18, stride=CROW), :] = edge[96:114, lanes]

    pooled = []
    for h in range(2):
        back = dot_nt(wb_ref[...], coarse_patch(ct, h * 8, 8)).astype(BF16).astype(F32) * 0.125
        total = jnp.zeros((256, 256), F32)
        for px in range(2):
            for py in range(2):
                pre = dot_nt(w1_ref[...], fine_patch(ft, h * 8, 8, px, py))
                act = leaky_rounded(pre)
                total = total + act[0:256] + act[256:512]
                both = jnp.concatenate([back, back], axis=0)
                bpre[px * 2 + py, :, h * 256 : h * 256 + 256] = jnp.where(pre > 0, both, LEAK * both).astype(BF16)
        mean = total * 0.125
        pooled.append(mean.astype(BF16))
        cells = mean.T.astype(BF16).astype(F32)
        for x in range(8):
            at = (h * 8 + x + 1) * CROW + 8
            for half in range(2):
                pp[half, at : at + HY, :] = cells[x * HY : x * HY + HY, half * 128 : half * 128 + 128]

    total = None
    for px in range(2):
        for py in range(2):
            part = dot_nn(bpre[px * 2 + py], fine_patch(ft, 0, HX, px, py))
            total = part if total is None else total + part
    g1[...] = total
    g2[...] = dot_nn(jnp.concatenate(pooled, axis=1), coarse_patch(ct, 0, HX))
    extract(g1, g2, grad_ref, a1, a2)

    coarse_taps(pp, pt)
    feat = dot_nt(coarse_patch(pt, 0, HX), w2_ref[...])
    feat_ref[...] = feat.astype(BF16).reshape(HX, HY, 256)


def final_kernel(scale, a_ref, b_ref, g1_ref, g2_ref):
    total = (a_ref[...] + b_ref[...]) * scale
    for kd in range(3):
        for kx in range(3):
            for ky in range(3):
                t = kd * 9 + kx * 3 + ky
                at = ((kx * 3 + ky) * 3 + kd) * 16
                g1_ref[t] = total[16:20, at : at + 16]
                at = (((2 - kx) * 3 + 2 - ky) * 3 + kd) * 16
                g2_ref[t] = total[0:16, at : at + 16]


def call(kernel, outs, scratch=()):
    return pl.pallas_call(
        kernel,
        out_shape=outs,
        scratch_shapes=list(scratch),
        compiler_params=pltpu.CompilerParams(vmem_limit_bytes=VMEM_LIMIT),
    )


def struct(shape, kind):
    return jax.ShapeDtypeStruct(shape, kind)


def swap(value, axis, step):
    n = lax.axis_size(axis)
    return lax.ppermute(value, axis, [(i, (i + step) % n) for i in range(n)])


def on_device(density, kernel_one, kernel_two, cotangent):
    d, c = density[0], cotangent[0]
    k1 = jnp.transpose(kernel_one, (2, 3, 4, 1, 0)).reshape(27, CIN, CH)
    k2 = jnp.transpose(kernel_two, (2, 3, 4, 0, 1)).reshape(27, CH, CH)

    message = struct((128, 128), BF16)
    up, down = call(
        pack_y_kernel, (message, message), (pltpu.VMEM((NXT * 16, 128), F32), pltpu.VMEM((2, HX * 16, 128), F32))
    )(d, c)
    lo, hi = swap(up, "ty", 1), swap(down, "ty", -1)
    w1, wb, w2 = call(
        weights_kernel,
        (struct((512, 1152), BF16), struct((256, 2304), BF16), struct((256, 2304), BF16)),
        (
            pltpu.VMEM((128, 128), F32),
            pltpu.VMEM((128, 128), F32),
            pltpu.VMEM((16, 27 * 128), F32),
            pltpu.VMEM((128, 2048), F32),
        ),
    )(k1, k2)
    message = struct((288, 128), BF16)
    up, down = call(
        pack_x_kernel,
        (message, message),
        (pltpu.VMEM((128, 128), F32), pltpu.VMEM((128, 128), F32), pltpu.VMEM((32, 128), F32)),
    )(d, c, lo, hi)
    xlo, xhi = swap(up, "tx", 1), swap(down, "tx", -1)

    feat, grads = call(
        main_kernel,
        (struct((HX, HY, 256), BF16), struct((24, 512), F32)),
        (
            pltpu.VMEM((40 * DROW, 128), F32),
            pltpu.VMEM((2, (HX + 2) * CROW, 128), F32),
            pltpu.VMEM((2, (HX + 2) * CROW, 128), F32),
            pltpu.VMEM((64, 128), F32),
            pltpu.VMEM((2, 20 * HY, 512), BF16),
            pltpu.VMEM(((HX + 2) * HY, 768), BF16),
            pltpu.VMEM(((HX + 2) * HY, 768), BF16),
            pltpu.VMEM((512, 1152), BF16),
            pltpu.VMEM((4, 512, 512), BF16),
            pltpu.VMEM((512, 1152), F32),
            pltpu.VMEM((256, 2304), F32),
            pltpu.VMEM((512, 128), F32),
            pltpu.VMEM((512, 256), F32),
        ),
    )(d, c, lo, hi, xlo, xhi, w1, wb, w2)

    steps = [(axis, k) for axis in ("ty", "tx", "rep") for k in (1, 2, 4) if k < lax.axis_size(axis)]
    other = jnp.zeros_like(grads)
    for at, (axis, k) in enumerate(steps):
        other = lax.ppermute(grads, axis, [(i, i ^ k) for i in range(lax.axis_size(axis))])
        if at < len(steps) - 1:
            grads = grads + other
    g1, g2 = call(
        functools.partial(final_kernel, 1.0 / lax.axis_size("rep")),
        (struct((27, CIN, CH), F32), struct((27, CH, CH), F32)),
    )(grads, other)
    g1 = jnp.transpose(g1.reshape(3, 3, 3, CIN, CH), (4, 3, 0, 1, 2))
    g2 = jnp.transpose(g2.reshape(3, 3, 3, CH, CH), (3, 4, 0, 1, 2))
    return feat[None], g1, g2


def solution(mesh):
    in_specs = (P("rep", "tx", "ty", None), P(), P(), P("rep", "tx", "ty", None))
    out_specs = (P("rep", "tx", "ty", None), P(), P())
    return jax.shard_map(on_device, mesh=mesh, in_specs=in_specs, out_specs=out_specs, check_vma=False)
```

```python
import jax
import jax.numpy as jnp
from jax import lax
from jax.experimental import pallas as pl
from jax.experimental.pallas import tpu as pltpu
from jax.sharding import Mesh
from jax.sharding import PartitionSpec as P

CIN = 4
CH = 16
LEAK = 0.3
F32 = jnp.float32
BF16 = jnp.bfloat16
NXT = 32
NYT = 64
HX = NXT // 2
HY = NYT // 2
DROW = 80
CROW = 48
ZONE = 10
VMEM_LIMIT = 32 * 1024 * 1024
FLOPS = 5_000_000_000
VMEM_ALL = 60 * 1024 * 1024


def dot_nt(lhs, rhs):
    return lax.dot_general(lhs, rhs, (((1,), (1,)), ((), ())), preferred_element_type=F32)


def dot_nn(lhs, rhs):
    return lax.dot_general(lhs, rhs, (((1,), (0,)), ((), ())), preferred_element_type=F32)


def iota(shape, dim):
    return lax.broadcasted_iota(jnp.int32, shape, dim)


def pack_y_kernel(d_hbm, c_hbm, up_ref, down_ref, db, cb, ds, cs, sem):
    copies = []
    for low in range(2):
        at, cat = (NYT - 16, HY - 16) if low == 0 else (0, 0)
        copies.append(pltpu.make_async_copy(d_hbm.at[:, pl.ds(at, 16), :], db.at[low], sem.at[2 * low]))
        copies.append(pltpu.make_async_copy(c_hbm.at[:, pl.ds(cat, 16), :], cb.at[low], sem.at[2 * low + 1]))
    for copy in copies:
        copy.start()
    for copy in copies:
        copy.wait()
    for low, out, row, crow in ((0, up_ref, 13, 15), (1, down_ref, 0, 0)):
        ds[...] = db[low].astype(F32).reshape(NXT * 16, 128)
        for half in range(2):
            cs[half] = cb[low, :, :, half * 128 : half * 128 + 128].astype(F32).reshape(HX * 16, 128)
        for k in range(3):
            out[k * 32 : k * 32 + 32, :] = ds[pl.ds(row + k, 32, stride=16), :].astype(BF16)
        for half in range(2):
            edge = cs[half, pl.ds(crow, 16, stride=16), :]
            out[96 + half * 16 : 112 + half * 16, :] = edge.astype(BF16)


def pack_x_kernel(d_ref, c_ref, lo_ref, hi_ref, after_ref, up_ref, down_ref, ls, hs, ms):
    ls[...] = lo_ref[...].astype(F32)
    hs[...] = hi_ref[...].astype(F32)
    for out, x, cx in ((down_ref, 0, 0), (up_ref, NXT - 3, HX - 1)):
        out[0:192, :] = d_ref[x : x + 3, :, :].reshape(192, 128)
        out[192:224, :] = c_ref[cx, :, 0:128]
        out[224:256, :] = c_ref[cx, :, 128:256]
        for side, src in enumerate((ls, hs)):
            for k in range(3):
                ms[side * 9 + 3 * k : side * 9 + 3 * k + 3, :] = src[k * 32 + x : k * 32 + x + 3, :]
            for half in range(2):
                at = 18 + side * 2 + half
                ms[at : at + 1, :] = src[96 + half * 16 + cx : 97 + half * 16 + cx, :]
        ms[22:32, :] = jnp.zeros((10, 128), F32)
        out[256:288, :] = ms[...].astype(BF16)


def weights_kernel(k1_ref, k2_ref, w1_ref, wb_ref, w2_ref, s1, so, c1, cf, cb):
    for t in range(27):
        s1[4 * t : 4 * t + 4, 0:CH] = k1_ref[t].astype(F32)
    s1[108:128, :] = jnp.zeros((20, 128), F32)
    k1t = s1[...].T[0:CH].astype(BF16)
    so[...] = jnp.zeros(so.shape, F32)
    for t in range(27):
        g, j = t // 8, t % 8
        so[g * 16 : g * 16 + 16, j * 16 : j * 16 + 16] = k2_ref[t].astype(F32)
    for g in range(4):
        for j in range(8):
            if g * 8 + j < 27:
                s1[j * 16 : j * 16 + 16, 0:CH] = k2_ref[g * 8 + j].astype(F32)
        so[64 + g * 16 : 80 + g * 16, :] = s1[...].T[0:CH]
    rep1 = (iota((128, 27 * 128), 0) == iota((128, 27 * 128), 1) // 32).astype(BF16)
    c1[...] = dot_nn(k1t, rep1)
    row, lane = iota((128, 2048), 0), iota((128, 2048), 1)
    rep2 = ((row // 16 == lane // 256) & (row % 16 == lane % 16)).astype(BF16)
    cf[...] = dot_nn(so[0:64, :].astype(BF16), rep2)
    rep2 = (row == lane // 16).astype(BF16)
    cb[...] = dot_nn(so[64:128, :].astype(BF16), rep2)

    depth1 = iota((16, 128), 1) % 32
    depth2 = iota((16, 256), 1) % 16
    gap = iota((1, 16, 256), 2) // 16 - iota((1, 16, 256), 1)
    for kx in range(3):
        for ky in range(3):
            ts = [kd * 9 + kx * 3 + ky for kd in range(3)]
            at = (kx * 3 + ky) * 128
            ones = [c1[:, t * 128 : t * 128 + 128] for t in ts]
            for d in range(32):
                acc = jnp.zeros((16, 128), F32)
                for kd in range(3):
                    acc = jnp.where(depth1 == d + kd - 1, ones[kd], acc)
                row = (d % 2) * 256 + (d // 2) * 16
                w1_ref[row : row + 16, at : at + 128] = acc.astype(BF16)
            at = ((2 - kx) * 3 + 2 - ky) * 256
            backs = [cb[t // 8 * 16 : t // 8 * 16 + 16, t % 8 * 256 : t % 8 * 256 + 256] for t in ts]
            for d in range(16):
                acc = jnp.zeros((16, 256), F32)
                for kd in range(3):
                    acc = jnp.where(depth2 == d + 1 - kd, backs[kd], acc)
                wb_ref[d * 16 : d * 16 + 16, at : at + 256] = acc.astype(BF16)
            at = (kx * 3 + ky) * 256
            acc = jnp.zeros((16, 16, 256), F32)
            for kd, t in enumerate(ts):
                part = cf[t // 8 * 16 : t // 8 * 16 + 16, t % 8 * 256 : t % 8 * 256 + 256]
                acc = jnp.where(gap == kd - 1, part[:, None, :], acc)
            w2_ref[:, at : at + 256] = acc.reshape(256, 256).astype(BF16)


def fine_taps(dp, taps, layers):
    for row, q, at in layers:
        for t in range(4):
            rows = dp[pl.ds(row + 7 + t, HY, stride=2), :]
            taps[q, at : at + HY, t * 128 : t * 128 + 128] = rows.astype(BF16)


def coarse_taps(padded, taps, count):
    for x in range(count):
        for k in range(3):
            for half in range(2):
                rows = padded[half, x * CROW + 7 + k : x * CROW + 7 + k + HY, :]
                lane = k * 256 + half * 128
                taps[x * HY : x * HY + HY, lane : lane + 128] = rows.astype(BF16)


def fine_patch(taps, first, count, px, py):
    parts = []
    for kx in range(3):
        s = px + kx - 1
        q = s % 2
        at = (first + (s - q) // 2) * HY
        parts.append(taps[q, at : at + count * HY, py * 128 : py * 128 + 384])
    return jnp.concatenate(parts, axis=1)


def coarse_patch(taps, first, count):
    parts = [taps[(first + k - 1) * HY : (first + k - 1 + count) * HY, :] for k in range(3)]
    return jnp.concatenate(parts, axis=1)


def pooled_sum(pre):
    total = jnp.zeros((256, 128), F32)
    for c in range(4):
        part = pre[:, c * 128 : c * 128 + 128]
        act = jnp.where(part > 0, part, LEAK * part).astype(BF16).astype(F32)
        total = total + act[0:256] + act[256:512]
    return total * 0.125


def back_through(pre, back):
    both = jnp.concatenate([back, back], axis=0)
    low = LEAK * both
    return [jnp.where(pre[:, c * 128 : c * 128 + 128] > 0, both, low).astype(BF16) for c in range(4)]


def inner_kernel(d_ref, c_ref, lo_ref, hi_ref, w1_ref, wb_ref, pool_ref, ct_ref, g1_ref, dp, cp, ft, bpre):
    for x in range(3, 29):
        at = (x - 3) * DROW + 8
        dp[at : at + NYT, :] = d_ref[x].astype(F32)
    for k in range(3):
        lo = lo_ref[k * 32 : k * 32 + 32, :].astype(F32)
        hi = hi_ref[k * 32 : k * 32 + 32, :].astype(F32)
        dp[pl.ds(5 + k, 26, stride=DROW), :] = lo[3:29]
        dp[pl.ds(8 + NYT + k, 26, stride=DROW), :] = hi[3:29]
    for half in range(2):
        for x in range(1, 15):
            at = (x - 1) * CROW + 8
            cp[half, at : at + HY, :] = c_ref[x, :, half * 128 : half * 128 + 128].astype(F32)
        rows = slice(96 + half * 16, 112 + half * 16)
        cp[half, pl.ds(7, 14, stride=CROW), :] = lo_ref[rows, :].astype(F32)[1:15]
        cp[half, pl.ds(8 + HY, 14, stride=CROW), :] = hi_ref[rows, :].astype(F32)[1:15]
    fine_taps(dp, ft, [((x - 3) * DROW, x % 2, (x // 2 - 1) * HY) for x in range(3, 29)])
    coarse_taps(cp, ct_ref, 14)
    back = dot_nt(wb_ref[...], coarse_patch(ct_ref, 1, 12)).astype(BF16).astype(F32) * 0.125
    patches = []
    for g in range(3):
        group = [fine_patch(ft, 1 + 4 * g, 4, px, py) for px in range(2) for py in range(2)]
        pre = dot_nt(w1_ref[...], jnp.concatenate(group, axis=0))
        pool_ref[:, g * 128 : g * 128 + 128] = pooled_sum(pre).astype(BF16)
        for c, part in enumerate(back_through(pre, back[:, g * 128 : g * 128 + 128])):
            bpre[:, (g * 4 + c) * 128 : (g * 4 + c) * 128 + 128] = part
        patches += group
    g1_ref[...] = dot_nn(bpre[...], jnp.concatenate(patches, axis=0))


def split_dot(select, values):
    high = values.astype(BF16)
    low = (values - high.astype(F32)).astype(BF16)
    return dot_nt(select, high) + dot_nt(select, low)


def extract(g1, g2, out_ref, a1, a2):
    depth1 = iota((16, 128), 1) % 32
    depth2 = iota((16, 256), 1) % 16
    for m in range(9):
        acc = [jnp.zeros((16, 128), F32)] * 3
        for d in range(32):
            row = (d % 2) * 256 + (d // 2) * 16
            part = g1[row : row + 16, m * 128 : m * 128 + 128]
            acc = [jnp.where(depth1 == d + kd - 1, part, acc[kd]) for kd in range(3)]
        for kd in range(3):
            a1[(m * 3 + kd) * 16 : (m * 3 + kd) * 16 + 16, :] = acc[kd]
        acc = [jnp.zeros((16, 256), F32)] * 3
        for d in range(16):
            part = g2[d * 16 : d * 16 + 16, m * 256 : m * 256 + 256]
            acc = [jnp.where(depth2 == d + 1 - kd, part, acc[kd]) for kd in range(3)]
        for kd in range(3):
            a2[(m * 3 + kd) * 16 : (m * 3 + kd) * 16 + 16, :] = acc[kd]
    a1[432:512, :] = jnp.zeros((80, 128), F32)
    a2[432:512, :] = jnp.zeros((80, 256), F32)
    pick2 = (iota((16, 256), 1) // 16 == iota((16, 256), 0)).astype(BF16)
    pick1 = (iota((16, 128), 1) // 32 == iota((16, 128), 0)).astype(BF16)
    two = split_dot(pick2, a2[...])
    one = split_dot(pick1, a1[...])
    out_ref[...] = jnp.concatenate([two, one], axis=0).astype(BF16)


def edge_kernel(
    d_ref, c_ref, lo_ref, hi_ref, xlo_ref, xhi_ref, w1_ref, wb_ref, pool_ref, ct_ref, g1_ref,
    grad_ref, rim_ref, ft, dp, cp, corner, ct, g1, g2, a1, a2,
):
    for zone, (src, base, first, own, x0) in enumerate(((xlo_ref, 1, 4, 0, -4), (xhi_ref, 6, 0, 26, 26))):
        top = zone * ZONE
        corner[zone * 32 : zone * 32 + 32, :] = src[256:288, :].astype(F32)
        for n in range(6):
            at = (top + first + n) * DROW + 8
            dp[at : at + NYT, :] = d_ref[own + n].astype(F32)
        for k in range(3):
            lo = lo_ref[k * 32 : k * 32 + 32, :].astype(F32)
            hi = hi_ref[k * 32 : k * 32 + 32, :].astype(F32)
            dp[pl.ds((top + first) * DROW + 5 + k, 6, stride=DROW), :] = lo[own : own + 6]
            dp[pl.ds((top + first) * DROW + 8 + NYT + k, 6, stride=DROW), :] = hi[own : own + 6]
            at = (top + base + k) * DROW + 8
            dp[at : at + NYT, :] = src[k * 64 : k * 64 + 64, :].astype(F32)
        for side, y in ((0, 5), (1, 8 + NYT)):
            for ky in range(3):
                for kx in range(3):
                    row = (top + base + kx) * DROW + y + ky
                    at = zone * 32 + side * 9 + 3 * ky + kx
                    dp[row : row + 1, :] = corner[at : at + 1, :]
        ctop, cbase, cfirst, cown = zone * 4, zone * 3, 1 - zone, zone * 13
        for half in range(2):
            lanes = slice(half * 128, half * 128 + 128)
            for n in range(3):
                at = (ctop + cfirst + n) * CROW + 8
                cp[half, at : at + HY, :] = c_ref[cown + n, :, lanes].astype(F32)
            rows = slice(96 + half * 16, 112 + half * 16)
            for side, y in ((0, 7), (1, 8 + HY)):
                part = (lo_ref, hi_ref)[side][rows, :].astype(F32)[cown : cown + 3]
                cp[half, pl.ds((ctop + cfirst) * CROW + y, 3, stride=CROW), :] = part
                row = (ctop + cbase) * CROW + y
                at = zone * 32 + 18 + side * 2 + half
                cp[half, row : row + 1, :] = corner[at : at + 1, :]
            at = (ctop + cbase) * CROW + 8
            cp[half, at : at + HY, :] = src[192 + half * 32 : 224 + half * 32, :].astype(F32)
    layers = []
    for n in range(2 * ZONE):
        if n not in (0, 2 * ZONE - 1):
            layers.append((n * DROW, n % 2, n // 2 * HY))
    fine_taps(dp, ft, layers)
    coarse_taps(cp, ct, 8)
    cpatch = jnp.concatenate([coarse_patch(ct, 1, 2), coarse_patch(ct, 5, 2)], axis=0)
    back = dot_nt(wb_ref[...], cpatch).astype(BF16).astype(F32) * 0.125
    group = []
    for px in range(2):
        for py in range(2):
            group += [fine_patch(ft, 2, 2, px, py), fine_patch(ft, 6, 2, px, py)]
    group = jnp.concatenate(group, axis=0)
    pre = dot_nt(w1_ref[...], group)
    mean = pooled_sum(pre).astype(BF16)
    rim_ref[...] = mean
    g1[...] = g1_ref[...] + dot_nn(jnp.concatenate(back_through(pre, back), axis=1), group)
    pooled = jnp.concatenate([pool_ref[...], mean], axis=1)
    g2[...] = dot_nn(pooled, jnp.concatenate([coarse_patch(ct_ref, 1, 12), cpatch], axis=0))
    extract(g1, g2, grad_ref, a1, a2)


def feature_kernel(
    after_ref, up_ref, down_ref, lo_ref, hi_ref, xlo_ref, xhi_ref, ft_ref, pool_ref, rim_ref, w1_ref, w2_ref,
    feat_ref, token_ref, col, corner, rim, pp, pt,
):
    for k in range(3):
        col[k, 8:40, :] = lo_ref[k * 32 : k * 32 + 32, :].astype(F32)
        col[5 + k, 8:40, :] = hi_ref[k * 32 : k * 32 + 32, :].astype(F32)
    col[3, 8:40, :] = down_ref[0:32, :].astype(F32)
    col[4, 8:40, :] = up_ref[64:96, :].astype(F32)
    for src, row in ((xlo_ref, 5), (xhi_ref, 40)):
        corner[...] = src[...].astype(F32)
        for kx in range(3):
            for ky in range(3):
                col[ky, row + kx : row + kx + 1, :] = corner[256 + 3 * ky + kx : 257 + 3 * ky + kx, :]
                col[5 + ky, row + kx : row + kx + 1, :] = corner[265 + 3 * ky + kx : 266 + 3 * ky + kx, :]
            col[3, row + kx : row + kx + 1, :] = corner[kx * 64 : kx * 64 + 1, :]
            col[4, row + kx : row + kx + 1, :] = corner[kx * 64 + 63 : kx * 64 + 64, :]
    for px in range(2):
        for py in range(2):
            at = (px * 2 + py) * 128
            rim[at : at + 32, :] = fine_patch(ft_ref, 1, 1, px, py)
            rim[at + 32 : at + 64, :] = fine_patch(ft_ref, 8, 1, px, py)
            for side in range(2):
                for kx in range(3):
                    for ky in range(3):
                        rows = col[side * 4 + py + ky, pl.ds(5 + px + kx, 18, stride=2), :]
                        rows = jnp.concatenate([rows, jnp.zeros((14, 128), F32)], axis=0)
                        lane = (kx * 3 + ky) * 128
                        rim[at + 64 + side * 32 : at + 96 + side * 32, lane : lane + 128] = rows.astype(BF16)
    edge = pooled_sum(dot_nt(w1_ref[...], rim[...])).T.astype(BF16).astype(F32)
    inner = pool_ref[...].astype(F32).T
    outer = rim_ref[...].astype(F32).T
    for half in range(2):
        lanes = slice(half * 128, half * 128 + 128)
        pp[half, 8:40, :] = edge[0:32, lanes]
        pp[half, (HX + 1) * CROW + 8 : (HX + 1) * CROW + 40, :] = edge[32:64, lanes]
        for n, x in enumerate((0, 1, 14, 15)):
            pp[half, (x + 1) * CROW + 8 : (x + 1) * CROW + 40, :] = outer[n * 32 : n * 32 + 32, lanes]
        for n in range(12):
            pp[half, (n + 3) * CROW + 8 : (n + 3) * CROW + 40, :] = inner[n * 32 : n * 32 + 32, lanes]
        pp[half, pl.ds(7, 18, stride=CROW), :] = edge[64:82, lanes]
        pp[half, pl.ds(8 + HY, 18, stride=CROW), :] = edge[96:114, lanes]
    coarse_taps(pp, pt, HX + 2)
    feat = dot_nt(coarse_patch(pt, 1, HX), w2_ref[...])
    feat_ref[...] = feat.astype(BF16).reshape(HX, HY, 256)
    token_ref[...] = feat[0:8, 0:128]


def add_two_kernel(a_ref, b_ref, out_ref):
    out_ref[...] = (a_ref[...].astype(F32) + b_ref[...].astype(F32)).astype(BF16)


def add_four(refs):
    a, b, c, d = (ref[...].astype(F32) for ref in refs)
    return (a + b) + (c + d)


def add_four_kernel(a_ref, b_ref, c_ref, d_ref, after_ref, out_ref):
    out_ref[...] = add_four((a_ref, b_ref, c_ref, d_ref)).astype(BF16)


def final_kernel(a_ref, b_ref, c_ref, d_ref, g1_ref, g2_ref):
    total = add_four((a_ref, b_ref, c_ref, d_ref)) * 0.5
    for kd in range(3):
        for kx in range(3):
            for ky in range(3):
                t = kd * 9 + kx * 3 + ky
                at = ((kx * 3 + ky) * 3 + kd) * 16
                g1_ref[t] = total[16:20, at : at + 16]
                at = (((2 - kx) * 3 + 2 - ky) * 3 + kd) * 16
                g2_ref[t] = total[0:16, at : at + 16]


ANY = pl.BlockSpec(memory_space=pl.ANY)
VM = pl.BlockSpec(memory_space=pltpu.VMEM)


def call(kernel, ins, outs, scratch=(), limit=VMEM_LIMIT, flops=None):
    cost = None if flops is None else pl.CostEstimate(flops=flops, bytes_accessed=1_000_000, transcendentals=0)
    return pl.pallas_call(
        kernel,
        out_shape=outs,
        in_specs=ins,
        scratch_shapes=list(scratch),
        cost_estimate=cost,
        compiler_params=pltpu.CompilerParams(vmem_limit_bytes=limit),
    )


def struct(shape, kind):
    return jax.ShapeDtypeStruct(shape, kind)


def buffer(*shape):
    return pltpu.VMEM(shape, F32)


def buffer16(*shape):
    return pltpu.VMEM(shape, BF16)


def shift(value, axes, step):
    n = lax.axis_size(axes)
    return lax.ppermute(value, axes, [(i, (i + step) % n) for i in range(n)])


def partner(value, axes, bits):
    n = lax.axis_size(axes)
    return lax.ppermute(value, axes, [(i, i ^ bits) for i in range(n)])


TX = ("x", "yh")
TY = ("z", "core")


def on_device(density, kernel_one, kernel_two, cotangent):
    d, c = density[0], cotangent[0]
    k1 = jnp.transpose(kernel_one, (2, 3, 4, 1, 0)).reshape(27, CIN, CH)
    k2 = jnp.transpose(kernel_two, (2, 3, 4, 0, 1)).reshape(27, CH, CH)

    message = struct((128, 128), BF16)
    yup, ydown = call(
        pack_y_kernel,
        [ANY] * 2,
        (message, message),
        (
            buffer16(2, NXT, 16, 128), buffer16(2, HX, 16, 256),
            buffer(NXT * 16, 128), buffer(2, HX * 16, 128), pltpu.SemaphoreType.DMA((4,)),
        ),
        limit=VMEM_ALL,
        flops=FLOPS,
    )(d, c)
    lo, hi = shift(yup, TY, 1), shift(ydown, TY, -1)
    w1, wb, w2 = call(
        weights_kernel,
        [VM] * 2,
        (struct((512, 1152), BF16), struct((256, 2304), BF16), struct((256, 2304), BF16)),
        (buffer(128, 128), buffer(128, 128), buffer(16, 27 * 128), buffer(64, 2048), buffer(64, 2048)),
    )(k1, k2)
    message = struct((288, 128), BF16)
    up, down = call(
        pack_x_kernel,
        [VM] * 4 + [ANY],
        (message, message),
        (buffer(128, 128), buffer(128, 128), buffer(32, 128)),
    )(d, c, lo, hi, w1)
    xlo, xhi = shift(up, TX, 1), shift(down, TX, -1)

    pool, ct, g1 = call(
        inner_kernel,
        [VM] * 6,
        (struct((256, 384), BF16), struct((14 * HY, 768), BF16), struct((512, 1152), F32)),
        (buffer(26 * DROW, 128), buffer(2, 14 * CROW, 128), buffer16(2, 14 * HY, 512), buffer16(512, 1536)),
    )(d, c, lo, hi, w1, wb)
    grads, rim, ft = call(
        edge_kernel,
        [VM] * 11,
        (struct((32, 512), BF16), struct((256, 128), BF16), struct((2, 10 * HY, 512), BF16)),
        (
            buffer(2 * ZONE * DROW, 128), buffer(2, 8 * CROW, 128), buffer(64, 128), buffer16(8 * HY, 768),
            buffer(512, 1152), buffer(256, 2304), buffer(512, 128), buffer(512, 256),
        ),
    )(d, c, lo, hi, xlo, xhi, w1, wb, pool, ct, g1)

    grads = call(add_two_kernel, [VM] * 2, struct((32, 512), BF16))(grads, partner(grads, "core", 1))
    feat, token = call(
        feature_kernel,
        [ANY] + [VM] * 11,
        (struct((HX, HY, 256), BF16), struct((8, 128), F32)),
        (
            buffer(8, 48, 128), buffer(288, 128), buffer16(512, 1152),
            buffer(2, (HX + 2) * CROW, 128), buffer16((HX + 2) * HY, 768),
        ),
    )(grads, yup, ydown, lo, hi, xlo, xhi, ft, pool, rim, w1, w2)
    after = w1
    for axes in ("z", "x"):
        others = [partner(grads, axes, bits) for bits in (1, 2, 3)]
        grads = call(add_four_kernel, [VM] * 4 + [ANY], struct((32, 512), BF16))(grads, *others, after)
        after = token
    near = partner(grads, "rep", 1)
    far, across = partner(grads, "yh", 1), partner(grads, ("rep", "yh"), 3)
    g1, g2 = call(final_kernel, [VM] * 4, (struct((27, CIN, CH), F32), struct((27, CH, CH), F32)))(
        grads, near, far, across
    )
    g1 = jnp.transpose(g1.reshape(3, 3, 3, CIN, CH), (4, 3, 0, 1, 2))
    g2 = jnp.transpose(g2.reshape(3, 3, 3, CH, CH), (3, 4, 0, 1, 2))
    return feat[None], g1, g2


def solution(mesh):
    fine = Mesh(mesh.devices.reshape(2, 4, 2, 4, 2), ("rep", "x", "yh", "z", "core"))
    tiles = P("rep", TX, TY, None)
    return jax.shard_map(
        on_device, mesh=fine, in_specs=(tiles, P(), P(), tiles), out_specs=(tiles, P(), P()), check_vma=False
    )
```

```python
import jax
import jax.numpy as jnp
from jax import lax
from jax.experimental import pallas as pl
from jax.experimental.pallas import tpu as pltpu
from jax.sharding import Mesh
from jax.sharding import PartitionSpec as P

CIN = 4
CH = 16
LEAK = 0.3
F32 = jnp.float32
BF16 = jnp.bfloat16
NXT = 32
NYT = 64
HX = NXT // 2
HY = NYT // 2
DROW = 80
CROW = 48
INNER = tuple(range(2, HX - 2))
OUTER = (0, 1, HX - 2, HX - 1)
VMEM_LIMIT = 32 * 1024 * 1024
FLOPS = 5_000_000_000
VMEM_ALL = 60 * 1024 * 1024


def dot_nt(lhs, rhs):
    return lax.dot_general(lhs, rhs, (((1,), (1,)), ((), ())), preferred_element_type=F32)


def dot_nn(lhs, rhs):
    return lax.dot_general(lhs, rhs, (((1,), (0,)), ((), ())), preferred_element_type=F32)


def iota(shape, dim):
    return lax.broadcasted_iota(jnp.int32, shape, dim)


def pack_y_kernel(d_hbm, c_hbm, up_ref, down_ref, db, cb, ds, cs, sem):
    copies = []
    for low in range(2):
        at, cat = (NYT - 16, HY - 16) if low == 0 else (0, 0)
        copies.append(pltpu.make_async_copy(d_hbm.at[:, pl.ds(at, 16), :], db.at[low], sem.at[2 * low]))
        copies.append(pltpu.make_async_copy(c_hbm.at[:, pl.ds(cat, 16), :], cb.at[low], sem.at[2 * low + 1]))
    for copy in copies:
        copy.start()
    for copy in copies:
        copy.wait()
    for low, out, row, crow in ((0, up_ref, 13, 15), (1, down_ref, 0, 0)):
        ds[...] = db[low].astype(F32).reshape(NXT * 16, 128)
        for half in range(2):
            cs[half] = cb[low, :, :, half * 128 : half * 128 + 128].astype(F32).reshape(HX * 16, 128)
        for k in range(3):
            out[k * 32 : k * 32 + 32, :] = ds[pl.ds(row + k, 32, stride=16), :].astype(BF16)
        for half in range(2):
            edge = cs[half, pl.ds(crow, 16, stride=16), :]
            out[96 + half * 16 : 112 + half * 16, :] = edge.astype(BF16)


def pack_x_kernel(d_ref, c_ref, lo_ref, hi_ref, after_ref, also_ref, up_ref, down_ref, ls, hs, ms):
    ls[...] = lo_ref[...].astype(F32)
    hs[...] = hi_ref[...].astype(F32)
    for out, x, cx in ((down_ref, 0, 0), (up_ref, NXT - 3, HX - 1)):
        out[0:192, :] = d_ref[x : x + 3, :, :].reshape(192, 128)
        out[192:224, :] = c_ref[cx, :, 0:128]
        out[224:256, :] = c_ref[cx, :, 128:256]
        for side, src in enumerate((ls, hs)):
            for k in range(3):
                ms[side * 9 + 3 * k : side * 9 + 3 * k + 3, :] = src[k * 32 + x : k * 32 + x + 3, :]
            for half in range(2):
                at = 18 + side * 2 + half
                ms[at : at + 1, :] = src[96 + half * 16 + cx : 97 + half * 16 + cx, :]
        ms[22:32, :] = jnp.zeros((10, 128), F32)
        out[256:288, :] = ms[...].astype(BF16)


def weights_kernel(k1_ref, k2_ref, w1_ref, wb_ref, s1, c1, cb):
    for t in range(27):
        s1[4 * t : 4 * t + 4, 0:CH] = k1_ref[t].astype(F32)
    s1[108:128, :] = jnp.zeros((20, 128), F32)
    k1t = s1[...].T[0:CH].astype(BF16)
    rep1 = (iota((128, 27 * 128), 0) == iota((128, 27 * 128), 1) // 32).astype(BF16)
    c1[...] = dot_nn(k1t, rep1)
    groups = []
    for g in range(4):
        for j in range(8):
            if g * 8 + j < 27:
                s1[j * 16 : j * 16 + 16, 0:CH] = k2_ref[g * 8 + j].astype(F32)
        groups.append(s1[...].T[0:CH])
    rep2 = (iota((128, 2048), 0) == iota((128, 2048), 1) // 16).astype(BF16)
    cb[...] = dot_nn(jnp.concatenate(groups, axis=0).astype(BF16), rep2)

    depth1 = iota((16, 128), 1) % 32
    depth2 = iota((16, 256), 1) % 16
    for kx in range(3):
        for ky in range(3):
            ts = [kd * 9 + kx * 3 + ky for kd in range(3)]
            at = (kx * 3 + ky) * 128
            ones = [c1[:, t * 128 : t * 128 + 128] for t in ts]
            for d in range(32):
                acc = jnp.zeros((16, 128), F32)
                for kd in range(3):
                    acc = jnp.where(depth1 == d + kd - 1, ones[kd], acc)
                row = (d % 2) * 256 + (d // 2) * 16
                w1_ref[row : row + 16, at : at + 128] = acc.astype(BF16)
            at = ((2 - kx) * 3 + 2 - ky) * 256
            backs = [cb[t // 8 * 16 : t // 8 * 16 + 16, t % 8 * 256 : t % 8 * 256 + 256] for t in ts]
            for d in range(16):
                acc = jnp.zeros((16, 256), F32)
                for kd in range(3):
                    acc = jnp.where(depth2 == d + 1 - kd, backs[kd], acc)
                wb_ref[d * 16 : d * 16 + 16, at : at + 256] = acc.astype(BF16)


def feature_weights_kernel(k2_ref, after_ref, w2_ref, so, cf):
    so[...] = jnp.zeros(so.shape, F32)
    for t in range(27):
        g, j = t // 8, t % 8
        so[g * 16 : g * 16 + 16, j * 16 : j * 16 + 16] = k2_ref[t].astype(F32)
    row, lane = iota((128, 2048), 0), iota((128, 2048), 1)
    rep2 = ((row // 16 == lane // 256) & (row % 16 == lane % 16)).astype(BF16)
    cf[...] = dot_nn(so[...].astype(BF16), rep2)
    gap = iota((1, 16, 256), 2) // 16 - iota((1, 16, 256), 1)
    for m in range(9):
        acc = jnp.zeros((16, 16, 256), F32)
        for kd in range(3):
            t = kd * 9 + m
            part = cf[t // 8 * 16 : t // 8 * 16 + 16, t % 8 * 256 : t % 8 * 256 + 256]
            acc = jnp.where(gap == kd - 1, part[:, None, :], acc)
        w2_ref[:, m * 256 : m * 256 + 256] = acc.reshape(256, 256).astype(BF16)


def fine_taps(dp, taps, layers):
    for n in range(layers):
        for t in range(4):
            rows = dp[pl.ds(n * DROW + 7 + t, HY, stride=2), :]
            taps[n * HY : n * HY + HY, t * 128 : t * 128 + 128] = rows.astype(BF16)


def coarse_taps(padded, taps, layers):
    for n in range(layers):
        for k in range(3):
            for half in range(2):
                rows = padded[half, n * CROW + 7 + k : n * CROW + 7 + k + HY, :]
                lane = k * 256 + half * 128
                taps[n * HY : n * HY + HY, lane : lane + 128] = rows.astype(BF16)


def fine_layer(taps, rims, x, py):
    if 0 <= x < NXT:
        return taps[x * HY : x * HY + HY, py * 128 : py * 128 + 384]
    n = x + 3 if x < 0 else x - NXT + 3
    return rims[n * HY : n * HY + HY, py * 128 : py * 128 + 384]


def fine_patch(taps, rims, cells, px, py):
    rows = []
    for cell in cells:
        rows.append(jnp.concatenate([fine_layer(taps, rims, 2 * cell + px + kx - 1, py) for kx in range(3)], axis=1))
    return jnp.concatenate(rows, axis=0)


def coarse_patch(taps, rims, cells):
    rows = []
    for cell in cells:
        parts = []
        for x in (cell - 1, cell, cell + 1):
            ref, n = (taps, x) if 0 <= x < HX else (rims, 0 if x < 0 else 1)
            parts.append(ref[n * HY : n * HY + HY, :])
        rows.append(jnp.concatenate(parts, axis=1))
    return jnp.concatenate(rows, axis=0)


def pooled_sum(pre):
    total = jnp.zeros((256, 128), F32)
    for c in range(4):
        part = pre[:, c * 128 : c * 128 + 128]
        act = jnp.where(part > 0, part, LEAK * part).astype(BF16).astype(F32)
        total = total + act[0:256] + act[256:512]
    return total * 0.125


def back_through(pre, back):
    both = jnp.concatenate([back, back], axis=0)
    low = LEAK * both
    return [jnp.where(pre[:, c * 128 : c * 128 + 128] > 0, both, low).astype(BF16) for c in range(4)]


def tap_kernel(d_ref, c_ref, ft_ref, ct_ref, dp, cp):
    for x in range(NXT):
        dp[x * DROW + 8 : x * DROW + 8 + NYT, :] = d_ref[x].astype(F32)
    for half in range(2):
        for x in range(HX):
            at = x * CROW + 8
            cp[half, at : at + HY, :] = c_ref[x, :, half * 128 : half * 128 + 128].astype(F32)
    fine_taps(dp, ft_ref, NXT)
    coarse_taps(cp, ct_ref, HX)


def set_row(ref, block, lanes, row, value):
    old = ref[block : block + 16, lanes].astype(F32)
    ref[block : block + 16, lanes] = jnp.where(iota((16, 128), 0) == row, value, old).astype(BF16)


def inner_kernel(ft_in, ct_in, lo_ref, hi_ref, w1_ref, wb_ref, ft, ct, pool_ref, g1_ref, ls, hs, bpre):
    ls[...] = lo_ref[...].astype(F32)
    hs[...] = hi_ref[...].astype(F32)
    for x in range(NXT):
        set_row(ft, x * HY, slice(0, 128), 0, ls[64 + x : 65 + x, :])
        set_row(ft, x * HY + 16, slice(384, 512), 15, hs[x : x + 1, :])
    for x in range(HX):
        for half in range(2):
            at = 96 + half * 16 + x
            set_row(ct, x * HY, slice(half * 128, half * 128 + 128), 0, ls[at : at + 1, :])
            set_row(ct, x * HY + 16, slice(512 + half * 128, 640 + half * 128), 15, hs[at : at + 1, :])
    back = dot_nt(wb_ref[...], coarse_patch(ct, None, INNER)).astype(BF16).astype(F32) * 0.125
    patches = []
    for g in range(3):
        cells = INNER[4 * g : 4 * g + 4]
        group = [fine_patch(ft, None, cells, px, py) for px in range(2) for py in range(2)]
        pre = dot_nt(w1_ref[...], jnp.concatenate(group, axis=0))
        pool_ref[:, g * 128 : g * 128 + 128] = pooled_sum(pre).astype(BF16)
        for c, part in enumerate(back_through(pre, back[:, g * 128 : g * 128 + 128])):
            bpre[:, (g * 4 + c) * 128 : (g * 4 + c) * 128 + 128] = part
        patches += group
    g1_ref[...] = dot_nn(bpre[...], jnp.concatenate(patches, axis=0))


def split_dot(select, values):
    high = values.astype(BF16)
    low = (values - high.astype(F32)).astype(BF16)
    return dot_nt(select, high) + dot_nt(select, low)


def extract(g1, g2, out_ref, a1, a2):
    depth1 = iota((16, 128), 1) % 32
    depth2 = iota((16, 256), 1) % 16
    for m in range(9):
        acc = [jnp.zeros((16, 128), F32)] * 3
        for d in range(32):
            row = (d % 2) * 256 + (d // 2) * 16
            part = g1[row : row + 16, m * 128 : m * 128 + 128]
            acc = [jnp.where(depth1 == d + kd - 1, part, acc[kd]) for kd in range(3)]
        for kd in range(3):
            a1[(m * 3 + kd) * 16 : (m * 3 + kd) * 16 + 16, :] = acc[kd]
        acc = [jnp.zeros((16, 256), F32)] * 3
        for d in range(16):
            part = g2[d * 16 : d * 16 + 16, m * 256 : m * 256 + 256]
            acc = [jnp.where(depth2 == d + 1 - kd, part, acc[kd]) for kd in range(3)]
        for kd in range(3):
            a2[(m * 3 + kd) * 16 : (m * 3 + kd) * 16 + 16, :] = acc[kd]
    a1[432:512, :] = jnp.zeros((80, 128), F32)
    a2[432:512, :] = jnp.zeros((80, 256), F32)
    pick2 = (iota((16, 256), 1) // 16 == iota((16, 256), 0)).astype(BF16)
    pick1 = (iota((16, 128), 1) // 32 == iota((16, 128), 0)).astype(BF16)
    two = split_dot(pick2, a2[...])
    one = split_dot(pick1, a1[...])[0:8]
    out_ref[...] = jnp.concatenate([two, one], axis=0).astype(BF16)


def edge_kernel(
    ft, ct, xlo_ref, xhi_ref, w1_ref, wb_ref, pool_ref, g1_ref,
    grad_ref, outer_ref, rims, dp, cp, corner, crims, g1, g2, a1, a2,
):
    for zone, src in enumerate((xlo_ref, xhi_ref)):
        corner[zone * 32 : zone * 32 + 32, :] = src[256:288, :].astype(F32)
        for k in range(3):
            at = (zone * 3 + k) * DROW + 8
            dp[at : at + NYT, :] = src[k * 64 : k * 64 + 64, :].astype(F32)
        for side, y in ((0, 5), (1, 8 + NYT)):
            for ky in range(3):
                for kx in range(3):
                    row = (zone * 3 + kx) * DROW + y + ky
                    at = zone * 32 + side * 9 + 3 * ky + kx
                    dp[row : row + 1, :] = corner[at : at + 1, :]
        for half in range(2):
            at = zone * CROW + 8
            cp[half, at : at + HY, :] = src[192 + half * 32 : 224 + half * 32, :].astype(F32)
            for side, y in ((0, 7), (1, 8 + HY)):
                at = zone * 32 + 18 + side * 2 + half
                cp[half, zone * CROW + y : zone * CROW + y + 1, :] = corner[at : at + 1, :]
    fine_taps(dp, rims, 6)
    coarse_taps(cp, crims, 2)
    cpatch = coarse_patch(ct, crims, OUTER)
    back = dot_nt(wb_ref[...], cpatch).astype(BF16).astype(F32) * 0.125
    group = [fine_patch(ft, rims, OUTER, px, py) for px in range(2) for py in range(2)]
    group = jnp.concatenate(group, axis=0)
    pre = dot_nt(w1_ref[...], group)
    mean = pooled_sum(pre).astype(BF16)
    outer_ref[...] = mean
    g1[...] = g1_ref[...] + dot_nn(jnp.concatenate(back_through(pre, back), axis=1), group)
    pooled = jnp.concatenate([pool_ref[...], mean], axis=1)
    g2[...] = dot_nn(pooled, jnp.concatenate([coarse_patch(ct, None, INNER), cpatch], axis=0))
    extract(g1, g2, grad_ref, a1, a2)


def rim_kernel(
    after_ref, up_ref, down_ref, lo_ref, hi_ref, xlo_ref, xhi_ref, ft_ref, rims_ref, w1_ref, edge_ref, col, corner, rim
):
    for k in range(3):
        col[k, 8:40, :] = lo_ref[k * 32 : k * 32 + 32, :].astype(F32)
        col[5 + k, 8:40, :] = hi_ref[k * 32 : k * 32 + 32, :].astype(F32)
    col[3, 8:40, :] = down_ref[0:32, :].astype(F32)
    col[4, 8:40, :] = up_ref[64:96, :].astype(F32)
    for src, row in ((xlo_ref, 5), (xhi_ref, 40)):
        corner[...] = src[...].astype(F32)
        for kx in range(3):
            for ky in range(3):
                col[ky, row + kx : row + kx + 1, :] = corner[256 + 3 * ky + kx : 257 + 3 * ky + kx, :]
                col[5 + ky, row + kx : row + kx + 1, :] = corner[265 + 3 * ky + kx : 266 + 3 * ky + kx, :]
            col[3, row + kx : row + kx + 1, :] = corner[kx * 64 : kx * 64 + 1, :]
            col[4, row + kx : row + kx + 1, :] = corner[kx * 64 + 63 : kx * 64 + 64, :]
    for px in range(2):
        for py in range(2):
            at = (px * 2 + py) * 128
            rim[at : at + 64, :] = fine_patch(ft_ref, rims_ref, (-1, HX), px, py)
            for side in range(2):
                for kx in range(3):
                    for ky in range(3):
                        rows = col[side * 4 + py + ky, pl.ds(5 + px + kx, 18, stride=2), :]
                        rows = jnp.concatenate([rows, jnp.zeros((14, 128), F32)], axis=0)
                        lane = (kx * 3 + ky) * 128
                        rim[at + 64 + side * 32 : at + 96 + side * 32, lane : lane + 128] = rows.astype(BF16)
    edge_ref[...] = pooled_sum(dot_nt(w1_ref[...], rim[...])).T.astype(BF16)


def feature_kernel(after_ref, edge_ref, pool_ref, outer_ref, w2_ref, feat_ref, token_ref, pp, pt):
    edge = edge_ref[...].astype(F32)
    inner = pool_ref[...].astype(F32).T
    outer = outer_ref[...].astype(F32).T
    for half in range(2):
        lanes = slice(half * 128, half * 128 + 128)
        pp[half, 8:40, :] = edge[0:32, lanes]
        pp[half, (HX + 1) * CROW + 8 : (HX + 1) * CROW + 40, :] = edge[32:64, lanes]
        for cells, part in ((INNER, inner), (OUTER, outer)):
            for n, x in enumerate(cells):
                pp[half, (x + 1) * CROW + 8 : (x + 1) * CROW + 40, :] = part[n * 32 : n * 32 + 32, lanes]
        pp[half, pl.ds(7, 18, stride=CROW), :] = edge[64:82, lanes]
        pp[half, pl.ds(8 + HY, 18, stride=CROW), :] = edge[96:114, lanes]
    coarse_taps(pp, pt, HX + 2)
    patch = [pt[k * HY : (k + HX) * HY, :] for k in range(3)]
    feat = dot_nt(jnp.concatenate(patch, axis=1), w2_ref[...])
    feat_ref[...] = feat.astype(BF16).reshape(HX, HY, 256)
    token_ref[...] = feat[0:8, 0:128]


def add_two_kernel(a_ref, b_ref, out_ref):
    out_ref[...] = (a_ref[...].astype(F32) + b_ref[...].astype(F32)).astype(BF16)


def add_four(refs):
    a, b, c, d = (ref[...].astype(F32) for ref in refs)
    return (a + b) + (c + d)


def add_four_kernel(a_ref, b_ref, c_ref, d_ref, after_ref, also_ref, out_ref):
    out_ref[...] = add_four((a_ref, b_ref, c_ref, d_ref)).astype(BF16)


def final_kernel(a_ref, b_ref, c_ref, d_ref, g1_ref, g2_ref):
    total = add_four((a_ref, b_ref, c_ref, d_ref)) * 0.5
    for kd in range(3):
        for kx in range(3):
            for ky in range(3):
                t = kd * 9 + kx * 3 + ky
                at = ((kx * 3 + ky) * 3 + kd) * 16
                g1_ref[t] = total[16:20, at : at + 16]
                at = (((2 - kx) * 3 + 2 - ky) * 3 + kd) * 16
                g2_ref[t] = total[0:16, at : at + 16]


ANY = pl.BlockSpec(memory_space=pl.ANY)
VM = pl.BlockSpec(memory_space=pltpu.VMEM)


def call(kernel, ins, outs, scratch=(), limit=VMEM_LIMIT, flops=None, aliases=None):
    cost = None if flops is None else pl.CostEstimate(flops=flops, bytes_accessed=1_000_000, transcendentals=0)
    return pl.pallas_call(
        kernel,
        out_shape=outs,
        in_specs=ins,
        scratch_shapes=list(scratch),
        cost_estimate=cost,
        input_output_aliases=aliases or {},
        compiler_params=pltpu.CompilerParams(vmem_limit_bytes=limit),
    )


def struct(shape, kind):
    return jax.ShapeDtypeStruct(shape, kind)


def buffer(*shape):
    return pltpu.VMEM(shape, F32)


def buffer16(*shape):
    return pltpu.VMEM(shape, BF16)


def shift(value, axes, step):
    n = lax.axis_size(axes)
    return lax.ppermute(value, axes, [(i, (i + step) % n) for i in range(n)])


def partner(value, axes, bits):
    n = lax.axis_size(axes)
    return lax.ppermute(value, axes, [(i, i ^ bits) for i in range(n)])


TX = ("x", "yh")
TY = ("z", "core")


def on_device(density, kernel_one, kernel_two, cotangent):
    d, c = density[0], cotangent[0]
    k1 = jnp.transpose(kernel_one, (2, 3, 4, 1, 0)).reshape(27, CIN, CH)
    k2 = jnp.transpose(kernel_two, (2, 3, 4, 0, 1)).reshape(27, CH, CH)

    message = struct((128, 128), BF16)
    yup, ydown = call(
        pack_y_kernel,
        [ANY] * 2,
        (message, message),
        (
            buffer16(2, NXT, 16, 128), buffer16(2, HX, 16, 256),
            buffer(NXT * 16, 128), buffer(2, HX * 16, 128), pltpu.SemaphoreType.DMA((4,)),
        ),
        limit=VMEM_ALL,
        flops=FLOPS,
    )(d, c)
    lo, hi = shift(yup, TY, 1), shift(ydown, TY, -1)
    w1, wb = call(
        weights_kernel,
        [VM] * 2,
        (struct((512, 1152), BF16), struct((256, 2304), BF16)),
        (buffer(128, 128), buffer(16, 27 * 128), buffer(64, 2048)),
    )(k1, k2)
    ft, ct = call(
        tap_kernel,
        [VM] * 2,
        (struct((NXT * HY, 512), BF16), struct((HX * HY, 768), BF16)),
        (buffer(NXT * DROW, 128), buffer(2, HX * CROW, 128)),
    )(d, c)
    message = struct((288, 128), BF16)
    up, down = call(
        pack_x_kernel,
        [VM] * 4 + [ANY] * 2,
        (message, message),
        (buffer(128, 128), buffer(128, 128), buffer(32, 128)),
    )(d, c, lo, hi, w1, ct)
    xlo, xhi = shift(up, TX, 1), shift(down, TX, -1)

    ft, ct, pool, g1 = call(
        inner_kernel,
        [VM] * 6,
        (struct(ft.shape, BF16), struct(ct.shape, BF16), struct((256, 384), BF16), struct((512, 1152), F32)),
        (buffer(128, 128), buffer(128, 128), buffer16(512, 1536)),
        aliases={0: 0, 1: 1},
    )(ft, ct, lo, hi, w1, wb)
    gradient = struct((24, 512), BF16)
    grads, outer, rims = call(
        edge_kernel,
        [VM] * 8,
        (gradient, struct((256, 128), BF16), struct((6 * HY, 512), BF16)),
        (
            buffer(6 * DROW, 128), buffer(2, 2 * CROW, 128), buffer(64, 128), buffer16(2 * HY, 768),
            buffer(512, 1152), buffer(256, 2304), buffer(512, 128), buffer(512, 256),
        ),
    )(ft, ct, xlo, xhi, w1, wb, pool, g1)

    grads = call(add_two_kernel, [VM] * 2, gradient)(grads, partner(grads, "core", 1))
    w2 = call(
        feature_weights_kernel,
        [VM, ANY],
        struct((256, 2304), BF16),
        (buffer(64, 128), buffer(64, 2048)),
    )(k2, grads)
    edge = call(
        rim_kernel,
        [ANY] + [VM] * 9,
        struct((128, 256), BF16),
        (buffer(8, 48, 128), buffer(288, 128), buffer16(512, 1152)),
    )(grads, yup, ydown, lo, hi, xlo, xhi, ft, rims, w1)
    others = [partner(grads, "z", bits) for bits in (1, 3, 2)]
    grads = call(add_four_kernel, [VM] * 4 + [ANY] * 2, gradient)(grads, *others, edge, w2)
    feat, token = call(
        feature_kernel,
        [ANY] + [VM] * 4,
        (struct((HX, HY, 256), BF16), struct((8, 128), F32)),
        (buffer(2, (HX + 2) * CROW, 128), buffer16((HX + 2) * HY, 768)),
    )(grads, edge, pool, outer, w2)
    others = [partner(grads, "x", bits) for bits in (1, 3, 2)]
    grads = call(add_four_kernel, [VM] * 4 + [ANY] * 2, gradient)(grads, *others, token, token)
    near = partner(grads, "rep", 1)
    across = partner(grads, ("rep", "yh"), 3)
    far = partner(grads, "yh", 1)
    g1, g2 = call(final_kernel, [VM] * 4, (struct((27, CIN, CH), F32), struct((27, CH, CH), F32)))(
        grads, near, across, far
    )
    g1 = jnp.transpose(g1.reshape(3, 3, 3, CIN, CH), (4, 3, 0, 1, 2))
    g2 = jnp.transpose(g2.reshape(3, 3, 3, CH, CH), (3, 4, 0, 1, 2))
    return feat[None], g1, g2


def solution(mesh):
    fine = Mesh(mesh.devices.reshape(2, 4, 2, 4, 2), ("rep", "x", "yh", "z", "core"))
    tiles = P("rep", TX, TY, None)
    return jax.shard_map(
        on_device, mesh=fine, in_specs=(tiles, P(), P(), tiles), out_specs=(tiles, P(), P()), check_vma=False
    )
```

```python
import jax
import jax.numpy as jnp
from jax import lax
from jax.experimental import pallas as pl
from jax.experimental.pallas import tpu as pltpu
from jax.sharding import Mesh
from jax.sharding import PartitionSpec as P

CIN = 4
CH = 16
LEAK = 0.3
F32 = jnp.float32
BF16 = jnp.bfloat16
NXT = 32
NYT = 64
HX = NXT // 2
HY = NYT // 2
DROW = 80
CROW = 48
INNER = tuple(range(2, HX - 2))
OUTER = (0, 1, HX - 2, HX - 1)
VMEM_LIMIT = 32 * 1024 * 1024
FLOPS = 5_000_000_000
VMEM_SPARE = 55050 * 1024


def dot_nt(lhs, rhs):
    return lax.dot_general(lhs, rhs, (((1,), (1,)), ((), ())), preferred_element_type=F32)


def dot_nn(lhs, rhs):
    return lax.dot_general(lhs, rhs, (((1,), (0,)), ((), ())), preferred_element_type=F32)


def iota(shape, dim):
    return lax.broadcasted_iota(jnp.int32, shape, dim)


def pack_y_kernel(d_hbm, c_hbm, up_ref, down_ref, db, cb, ds, cs, sem):
    copies = []
    for low in range(2):
        at, cat = (NYT - 16, HY - 16) if low == 0 else (0, 0)
        copies.append(pltpu.make_async_copy(d_hbm.at[:, pl.ds(at, 16), :], db.at[low], sem.at[2 * low]))
        copies.append(pltpu.make_async_copy(c_hbm.at[:, pl.ds(cat, 16), :], cb.at[low], sem.at[2 * low + 1]))
    for copy in copies:
        copy.start()
    for copy in copies:
        copy.wait()
    for low, out, row, crow in ((0, up_ref, 13, 15), (1, down_ref, 0, 0)):
        ds[...] = db[low].astype(F32).reshape(NXT * 16, 128)
        for half in range(2):
            cs[half] = cb[low, :, :, half * 128 : half * 128 + 128].astype(F32).reshape(HX * 16, 128)
        for k in range(3):
            out[k * 32 : k * 32 + 32, :] = ds[pl.ds(row + k, 32, stride=16), :].astype(BF16)
        for half in range(2):
            edge = cs[half, pl.ds(crow, 16, stride=16), :]
            out[96 + half * 16 : 112 + half * 16, :] = edge.astype(BF16)


def pack_x_kernel(d_ref, c_ref, lo_ref, hi_ref, after_ref, also_ref, up_ref, down_ref, ls, hs, ms):
    ls[...] = lo_ref[...].astype(F32)
    hs[...] = hi_ref[...].astype(F32)
    for out, x, cx in ((down_ref, 0, 0), (up_ref, NXT - 3, HX - 1)):
        out[0:192, :] = d_ref[x : x + 3, :, :].reshape(192, 128)
        out[192:224, :] = c_ref[cx, :, 0:128]
        out[224:256, :] = c_ref[cx, :, 128:256]
        for side, src in enumerate((ls, hs)):
            for k in range(3):
                ms[side * 9 + 3 * k : side * 9 + 3 * k + 3, :] = src[k * 32 + x : k * 32 + x + 3, :]
            for half in range(2):
                at = 18 + side * 2 + half
                ms[at : at + 1, :] = src[96 + half * 16 + cx : 97 + half * 16 + cx, :]
        ms[22:32, :] = jnp.zeros((10, 128), F32)
        out[256:288, :] = ms[...].astype(BF16)


def weights_kernel(k1_ref, k2_ref, w1_ref, wb_ref, s1, c1, cb):
    for t in range(27):
        s1[4 * t : 4 * t + 4, 0:CH] = k1_ref[t].astype(F32)
    s1[108:128, :] = jnp.zeros((20, 128), F32)
    k1t = s1[...].T[0:CH].astype(BF16)
    t27, i = iota((128, 128), 0) // 4, iota((128, 128), 0) % 4
    lane = iota((128, 128), 1)
    spread = []
    for kd in range(3):
        for b in range(5):
            tap = 2 * b + lane // 64
            spread.append((t27 == kd * 9 + tap) & (tap <= 8) & (i == lane % 64 // 16))
    u = lane - 64
    for h in range(2):
        for py in range(2):
            kx, ky = u // 16, u % 16 // 4 - py
            good = (u >= 0) & (kx <= 2) & (ky >= 0) & (ky <= 2) & (i == u % 4)
            spread.append((t27 == (2 - 2 * h) * 9 + kx * 3 + ky) & good)
    c1[...] = dot_nn(k1t, jnp.concatenate([part.astype(BF16) for part in spread], axis=1))
    groups = []
    for g in range(4):
        for j in range(8):
            if g * 8 + j < 27:
                s1[j * 16 : j * 16 + 16, 0:CH] = k2_ref[g * 8 + j].astype(F32)
        groups.append(s1[...].T[0:CH])
    rep2 = (iota((128, 2048), 0) == iota((128, 2048), 1) // 16).astype(BF16)
    cb[...] = dot_nn(jnp.concatenate(groups, axis=0).astype(BF16), rep2)

    depth1 = iota((16, 128), 1) % 16
    depth2 = iota((16, 256), 1) % 16
    for h in range(2):
        for n in range(16):
            row = (n % 2) * 128 + (n // 2) * 16
            touches = n == 15 - 15 * h
            for b in range(6):
                acc = jnp.zeros((16, 128), F32)
                if b < 5:
                    for kd in range(3):
                        at = (kd * 5 + b) * 128
                        acc = jnp.where(depth1 == n + kd - 1, c1[:, at : at + 128], acc)
                if b >= 4 and touches:
                    at = (15 + 2 * h + b - 4) * 128
                    acc = acc + c1[:, at : at + 128]
                w1_ref[h, row : row + 16, b * 128 : b * 128 + 128] = acc.astype(BF16)
    for kx in range(3):
        for ky in range(3):
            ts = [kd * 9 + kx * 3 + ky for kd in range(3)]
            at = ((2 - kx) * 3 + 2 - ky) * 256
            backs = [cb[t // 8 * 16 : t // 8 * 16 + 16, t % 8 * 256 : t % 8 * 256 + 256] for t in ts]
            for d in range(16):
                acc = jnp.zeros((16, 256), F32)
                for kd in range(3):
                    acc = jnp.where(depth2 == d + 1 - kd, backs[kd], acc)
                wb_ref[d * 16 : d * 16 + 16, at : at + 256] = acc.astype(BF16)


def feature_weights_kernel(k2_ref, after_ref, w2_ref, so, cf):
    so[...] = jnp.zeros(so.shape, F32)
    for t in range(27):
        g, j = t // 8, t % 8
        so[g * 16 : g * 16 + 16, j * 16 : j * 16 + 16] = k2_ref[t].astype(F32)
    row, lane = iota((128, 2048), 0), iota((128, 2048), 1)
    rep2 = ((row // 16 == lane // 256) & (row % 16 == lane % 16)).astype(BF16)
    cf[...] = dot_nn(so[...].astype(BF16), rep2)
    gap = iota((1, 16, 256), 2) // 16 - iota((1, 16, 256), 1)
    for m in range(9):
        acc = jnp.zeros((16, 16, 256), F32)
        for kd in range(3):
            t = kd * 9 + m
            part = cf[t // 8 * 16 : t // 8 * 16 + 16, t % 8 * 256 : t % 8 * 256 + 256]
            acc = jnp.where(gap == kd - 1, part[:, None, :], acc)
        w2_ref[:, m * 256 : m * 256 + 256] = acc.reshape(256, 256).astype(BF16)


def halves_matrix():
    row, col = iota((128, 256), 0), iota((128, 256), 1)
    place = row % 32 // 16 * 64 + row // 32 * 16 + row % 16
    return (place == (col + col // 128 * 64) % 128).astype(BF16)


def touch_matrix():
    row, col = iota((512, 256), 0), iota((512, 256), 1)
    u = col % 128 - 64
    lane = jnp.where(col < 128, 64 + u % 4 * 16, u % 4 * 16 + 15)
    return ((row // 128 == u % 16 // 4) & (row % 128 == lane) & (u >= 0)).astype(BF16)


def fine_taps(dp, ds, ft, fs, vt, layers):
    for n in range(layers):
        for t in range(4):
            for src, out in ((dp, ft), (ds, fs)):
                rows = src[pl.ds(n * DROW + 7 + t, HY, stride=2), :]
                out[n * HY : n * HY + HY, t * 128 : t * 128 + 128] = rows.astype(BF16)
    vt[...] = dot_nn(ft[...], touch_matrix()).astype(BF16)


def coarse_taps(padded, taps, layers):
    for n in range(layers):
        for k in range(3):
            for half in range(2):
                rows = padded[half, n * CROW + 7 + k : n * CROW + 7 + k + HY, :]
                lane = k * 256 + half * 128
                taps[n * HY : n * HY + HY, lane : lane + 128] = rows.astype(BF16)


def pick(low, first, second):
    return jnp.where(low, first, second)


def patch_blocks(h, py, plain, swapped, touch, rows):
    lane = iota((rows, 128), 1)
    low = lane < 64
    first, second = (plain, swapped) if h == 0 else (swapped, plain)
    blocks = [pick(low, first(2 * b // 3, 2 * b % 3), second((2 * b + 1) // 3, (2 * b + 1) % 3)) for b in range(4)]
    zero = jnp.zeros((rows, 128), BF16)
    edge = pick(lane < 80, touch(0), pick(lane < 96, touch(1), touch(2)))
    blocks.append(pick(low, first(2, 2), edge if py == 0 else zero))
    blocks.append(edge if py == 1 else zero)
    return blocks


def store_patch(out, h, at, fine, rims, cell, px, py):
    def layer(which, x, lanes):
        if 0 <= x < NXT:
            return fine[which][x * HY : x * HY + HY, lanes]
        n = x + 3 if x < 0 else x - NXT + 3
        return rims[which][n * HY : n * HY + HY, lanes]

    def tap(which):
        return lambda kx, ky: layer(which, 2 * cell + px + kx - 1, slice((py + ky) * 128, (py + ky) * 128 + 128))

    def touch(kx):
        return layer(2, 2 * cell + px + kx - 1, slice(h * 128, h * 128 + 128))

    for b, block in enumerate(patch_blocks(h, py, tap(0), tap(1), touch, HY)):
        out[h, at : at + HY, b * 128 : b * 128 + 128] = block


def coarse_patch(taps, rims, cells):
    rows = []
    for cell in cells:
        parts = []
        for x in (cell - 1, cell, cell + 1):
            ref, n = (taps, x) if 0 <= x < HX else (rims, 0 if x < 0 else 1)
            parts.append(ref[n * HY : n * HY + HY, :])
        rows.append(jnp.concatenate(parts, axis=1))
    return jnp.concatenate(rows, axis=0)


def pooled_sum(pres):
    parts = []
    for pre in pres:
        total = jnp.zeros((128, 128), F32)
        for c in range(4):
            part = pre[:, c * 128 : c * 128 + 128]
            act = jnp.where(part > 0, part, LEAK * part).astype(BF16).astype(F32)
            total = total + act[0:128] + act[128:256]
        parts.append(total * 0.125)
    return jnp.concatenate(parts, axis=0)


def back_through(h, pre, back):
    part = back[h * 128 : h * 128 + 128]
    both = jnp.concatenate([part, part], axis=0)
    low = LEAK * both
    return [jnp.where(pre[:, c * 128 : c * 128 + 128] > 0, both, low).astype(BF16) for c in range(4)]


def tap_kernel(d_ref, c_ref, ft_ref, fs_ref, vt_ref, ct_ref, dp, ds, cp):
    both = dot_nn(d_ref[...].reshape(NXT * NYT, 128), halves_matrix())
    for n, out in enumerate((dp, ds)):
        for x in range(NXT):
            out[x * DROW + 8 : x * DROW + 8 + NYT, :] = both[x * NYT : x * NYT + NYT, n * 128 : n * 128 + 128]
        for y in (7, 8 + NYT):
            out[pl.ds(y, NXT, stride=DROW), :] = jnp.zeros((NXT, 128), F32)
    for half in range(2):
        for x in range(HX):
            at = x * CROW + 8
            cp[half, at : at + HY, :] = c_ref[x, :, half * 128 : half * 128 + 128].astype(F32)
    fine_taps(dp, ds, ft_ref, fs_ref, vt_ref, NXT)
    coarse_taps(cp, ct_ref, HX)


def set_row(ref, block, lanes, row, value, tap=None):
    old = ref[block : block + 16, lanes].astype(F32)
    where = iota(old.shape, 0) == row
    if tap is not None:
        where = where & (iota(old.shape, 1) % 16 // 4 == tap)
    ref[block : block + 16, lanes] = jnp.where(where, value, old).astype(BF16)


def inner_kernel(
    ft_in, fs_in, vt_in, ct_in, lo_ref, hi_ref, w1_ref, wb_ref, ft, fs, vt, ct, pool_ref, g1_ref, ls, hs, ys, pa, bpre
):
    ls[...] = lo_ref[...].astype(F32)
    hs[...] = hi_ref[...].astype(F32)
    touch = touch_matrix()
    for n, rows, t in ((0, lo_ref[64:96, :], 0), (1, hi_ref[0:32, :], 3)):
        both = dot_nn(rows, halves_matrix())
        ys[n, :, 0:256] = both
        ys[n, :, 256:512] = dot_nn(both[:, 0:128].astype(BF16), touch[t * 128 : t * 128 + 128])
    for x in range(NXT):
        for n, block, row, t in ((0, x * HY, 0, 0), (1, x * HY + 16, 15, 3)):
            lanes = slice(t * 128, t * 128 + 128)
            set_row(ft, block, lanes, row, ys[n, x : x + 1, 0:128])
            set_row(fs, block, lanes, row, ys[n, x : x + 1, 128:256])
            set_row(vt, block, slice(0, 256), row, ys[n, x : x + 1, 256:512], t)
    for x in range(HX):
        for half in range(2):
            at = 96 + half * 16 + x
            set_row(ct, x * HY, slice(half * 128, half * 128 + 128), 0, ls[at : at + 1, :])
            set_row(ct, x * HY + 16, slice(512 + half * 128, 640 + half * 128), 15, hs[at : at + 1, :])
    back = dot_nt(wb_ref[...], coarse_patch(ct, None, INNER)).astype(BF16).astype(F32) * 0.125
    for g in range(3):
        for h in range(2):
            for c in range(4):
                for n in range(4):
                    at = (g * 4 + c) * 128 + n * HY
                    store_patch(pa, h, at, (ft, fs, vt), None, INNER[4 * g + n], c // 2, c % 2)
        pres = [dot_nt(w1_ref[h], pa[h, g * 512 : g * 512 + 512, :]) for h in range(2)]
        pool_ref[:, g * 128 : g * 128 + 128] = pooled_sum(pres).astype(BF16)
        for h in range(2):
            for c, part in enumerate(back_through(h, pres[h], back[:, g * 128 : g * 128 + 128])):
                bpre[h, :, (g * 4 + c) * 128 : (g * 4 + c) * 128 + 128] = part
    for h in range(2):
        g1_ref[h] = dot_nn(bpre[h], pa[h])


def split_dot(select, values):
    high = values.astype(BF16)
    low = (values - high.astype(F32)).astype(BF16)
    return dot_nt(select, high) + dot_nt(select, low)


def extract(g1, g2, out_ref, a1, a2):
    depth1 = iota((16, 128), 1) % 16
    depth2 = iota((16, 256), 1) % 16
    row, col = iota((256, 640), 0), iota((256, 640), 1)
    u = row % 128 - 64
    tap = u // 16 * 3 + u % 16 // 4 - row // 128
    ky = u % 16 // 4 - row // 128
    good = (u >= 0) & (u < 48) & (ky >= 0) & (ky <= 2)
    place = (good & (col == tap // 2 * 128 + tap % 2 * 64 + u % 4 * 16)).astype(BF16)
    touch = jnp.concatenate([g1[0, 240:256, 512:768], g1[1, 0:16, 512:768]], axis=0)
    high = touch.astype(BF16)
    touch = dot_nn(high, place) + dot_nn((touch - high.astype(F32)).astype(BF16), place)
    for b in range(5):
        lanes = slice(b * 128, b * 128 + 128)
        total = [touch[16:32, lanes], jnp.zeros((16, 128), F32), touch[0:16, lanes]]
        for h in range(2):
            acc = [jnp.zeros((16, 128), F32)] * 3
            for n in range(16):
                row = (n % 2) * 128 + (n // 2) * 16
                part = g1[h, row : row + 16, lanes]
                acc = [jnp.where(depth1 == n + kd - 1, part, acc[kd]) for kd in range(3)]
            total = [total[kd] + acc[kd] for kd in range(3)]
        for kd in range(3):
            a1[(b * 3 + kd) * 16 : (b * 3 + kd) * 16 + 16, :] = total[kd]
    for m in range(9):
        acc = [jnp.zeros((16, 256), F32)] * 3
        for d in range(16):
            part = g2[d * 16 : d * 16 + 16, m * 256 : m * 256 + 256]
            acc = [jnp.where(depth2 == d + 1 - kd, part, acc[kd]) for kd in range(3)]
        for kd in range(3):
            a2[(m * 3 + kd) * 16 : (m * 3 + kd) * 16 + 16, :] = acc[kd]
    a1[240:512, :] = jnp.zeros((272, 128), F32)
    a2[432:512, :] = jnp.zeros((80, 256), F32)
    pick2 = (iota((16, 256), 1) // 16 == iota((16, 256), 0)).astype(BF16)
    pick1 = (iota((16, 128), 1) // 16 == iota((16, 128), 0)).astype(BF16)
    two = split_dot(pick2, a2[...])
    one = split_dot(pick1, a1[...])[0:8]
    out_ref[...] = jnp.concatenate([two, one], axis=0).astype(BF16)


def edge_kernel(
    ft, fs, vt, ct, xlo_ref, xhi_ref, w1_ref, wb_ref, pool_ref, g1_ref,
    grad_ref, outer_ref, rft, rfs, rvt, dp, ds, cp, corner, swapped, crims, pa, g1, g2, a1, a2,
):
    for zone, src in enumerate((xlo_ref, xhi_ref)):
        both = dot_nn(jnp.concatenate([src[0:192, :], src[256:288, :]], axis=0), halves_matrix())
        for k in range(3):
            at = (zone * 3 + k) * DROW + 8
            dp[at : at + NYT, :] = both[k * 64 : k * 64 + 64, 0:128]
            ds[at : at + NYT, :] = both[k * 64 : k * 64 + 64, 128:256]
        swapped[0] = both[192:224, 0:128]
        swapped[1] = both[192:224, 128:256]
        corner[zone * 32 : zone * 32 + 32, :] = src[256:288, :].astype(F32)
        for side, y in ((0, 5), (1, 8 + NYT)):
            for ky in range(3):
                for kx in range(3):
                    row = (zone * 3 + kx) * DROW + y + ky
                    at = side * 9 + 3 * ky + kx
                    dp[row : row + 1, :] = swapped[0, at : at + 1, :]
                    ds[row : row + 1, :] = swapped[1, at : at + 1, :]
        for half in range(2):
            at = zone * CROW + 8
            cp[half, at : at + HY, :] = src[192 + half * 32 : 224 + half * 32, :].astype(F32)
            for side, y in ((0, 7), (1, 8 + HY)):
                at = zone * 32 + 18 + side * 2 + half
                cp[half, zone * CROW + y : zone * CROW + y + 1, :] = corner[at : at + 1, :]
    fine_taps(dp, ds, rft, rfs, rvt, 6)
    coarse_taps(cp, crims, 2)
    cpatch = coarse_patch(ct, crims, OUTER)
    back = dot_nt(wb_ref[...], cpatch).astype(BF16).astype(F32) * 0.125
    for h in range(2):
        for c in range(4):
            for n, cell in enumerate(OUTER):
                store_patch(pa, h, c * 128 + n * HY, (ft, fs, vt), (rft, rfs, rvt), cell, c // 2, c % 2)
    pres = [dot_nt(w1_ref[h], pa[h]) for h in range(2)]
    mean = pooled_sum(pres).astype(BF16)
    outer_ref[...] = mean
    for h in range(2):
        g1[h] = g1_ref[h] + dot_nn(jnp.concatenate(back_through(h, pres[h], back), axis=1), pa[h])
    pooled = jnp.concatenate([pool_ref[...], mean], axis=1)
    g2[...] = dot_nn(pooled, jnp.concatenate([coarse_patch(ct, None, INNER), cpatch], axis=0))
    extract(g1, g2, grad_ref, a1, a2)


def rim_kernel(
    after_ref, up_ref, down_ref, lo_ref, hi_ref, xlo_ref, xhi_ref, ft, fs, vt, rft, rfs, rvt, w1_ref,
    edge_ref, col, raw, corner, tv, rim,
):
    raw[...] = jnp.zeros(raw.shape, F32)
    for k in range(3):
        raw[k, 8:40, :] = lo_ref[k * 32 : k * 32 + 32, :].astype(F32)
        raw[5 + k, 8:40, :] = hi_ref[k * 32 : k * 32 + 32, :].astype(F32)
    raw[3, 8:40, :] = down_ref[0:32, :].astype(F32)
    raw[4, 8:40, :] = up_ref[64:96, :].astype(F32)
    for src, row in ((xlo_ref, 5), (xhi_ref, 40)):
        corner[...] = src[...].astype(F32)
        for kx in range(3):
            for ky in range(3):
                raw[ky, row + kx : row + kx + 1, :] = corner[256 + 3 * ky + kx : 257 + 3 * ky + kx, :]
                raw[5 + ky, row + kx : row + kx + 1, :] = corner[265 + 3 * ky + kx : 266 + 3 * ky + kx, :]
            raw[3, row + kx : row + kx + 1, :] = corner[kx * 64 : kx * 64 + 1, :]
            raw[4, row + kx : row + kx + 1, :] = corner[kx * 64 + 63 : kx * 64 + 64, :]
    both = dot_nn(raw[...].reshape(8 * 48, 128).astype(BF16), halves_matrix())
    touch = touch_matrix()
    for side in range(2):
        parts = []
        for t in range(4):
            part = both[(side * 4 + t) * 48 : (side * 4 + t) * 48 + 48]
            col[0, side * 4 + t] = part[:, 0:128]
            col[1, side * 4 + t] = part[:, 128:256]
            parts.append(part[:, 0:128].astype(BF16))
        ends = dot_nn(jnp.concatenate(parts, axis=1), touch)
        tv[side, 0] = ends[:, 0:128]
        tv[side, 1] = ends[:, 128:256]
    blank = jnp.zeros((14, 128), F32)
    for h in range(2):
        for px in range(2):
            for py in range(2):
                at = (px * 2 + py) * 128
                for n, cell in enumerate((-1, HX)):
                    store_patch(rim, h, at + n * HY, (ft, fs, vt), (rft, rfs, rvt), cell, px, py)
                for side in range(2):

                    def tap(which):
                        def get(kx, ky):
                            rows = col[which, side * 4 + py + ky, pl.ds(5 + px + kx, 18, stride=2), :]
                            return jnp.concatenate([rows, blank], axis=0).astype(BF16)

                        return get

                    def ends_of(kx):
                        rows = tv[side, h, pl.ds(5 + px + kx, 18, stride=2), :]
                        return jnp.concatenate([rows, blank], axis=0).astype(BF16)

                    top = at + 64 + side * 32
                    for b, block in enumerate(patch_blocks(h, py, tap(0), tap(1), ends_of, 32)):
                        rim[h, top : top + 32, b * 128 : b * 128 + 128] = block
    pres = [dot_nt(w1_ref[h], rim[h]) for h in range(2)]
    edge_ref[...] = pooled_sum(pres).T.astype(BF16)


def feature_kernel(after_ref, edge_ref, pool_ref, outer_ref, w2_ref, feat_ref, token_ref, pp, pt):
    edge = edge_ref[...].astype(F32)
    inner = pool_ref[...].astype(F32).T
    outer = outer_ref[...].astype(F32).T
    for half in range(2):
        lanes = slice(half * 128, half * 128 + 128)
        pp[half, 8:40, :] = edge[0:32, lanes]
        pp[half, (HX + 1) * CROW + 8 : (HX + 1) * CROW + 40, :] = edge[32:64, lanes]
        for cells, part in ((INNER, inner), (OUTER, outer)):
            for n, x in enumerate(cells):
                pp[half, (x + 1) * CROW + 8 : (x + 1) * CROW + 40, :] = part[n * 32 : n * 32 + 32, lanes]
        pp[half, pl.ds(7, 18, stride=CROW), :] = edge[64:82, lanes]
        pp[half, pl.ds(8 + HY, 18, stride=CROW), :] = edge[96:114, lanes]
    coarse_taps(pp, pt, HX + 2)
    patch = [pt[k * HY : (k + HX) * HY, :] for k in range(3)]
    feat = dot_nt(jnp.concatenate(patch, axis=1), w2_ref[...])
    feat_ref[...] = feat.astype(BF16).reshape(HX, HY, 256)
    token_ref[...] = feat[0:8, 0:128]


def add_two_kernel(a_ref, b_ref, out_ref):
    out_ref[...] = (a_ref[...].astype(F32) + b_ref[...].astype(F32)).astype(BF16)


def add_four(refs):
    a, b, c, d = (ref[...].astype(F32) for ref in refs)
    return (a + b) + (c + d)


def add_four_kernel(a_ref, b_ref, c_ref, d_ref, after_ref, also_ref, out_ref):
    out_ref[...] = add_four((a_ref, b_ref, c_ref, d_ref)).astype(BF16)


def final_kernel(a_ref, b_ref, c_ref, d_ref, g1_ref, g2_ref):
    total = add_four((a_ref, b_ref, c_ref, d_ref)) * 0.5
    for kd in range(3):
        for kx in range(3):
            for ky in range(3):
                t, m = kd * 9 + kx * 3 + ky, kx * 3 + ky
                at, row = (m // 2 * 3 + kd) * 16, 16 + m % 2 * 4
                g1_ref[t] = total[row : row + 4, at : at + 16]
                at = (((2 - kx) * 3 + 2 - ky) * 3 + kd) * 16
                g2_ref[t] = total[0:16, at : at + 16]


ANY = pl.BlockSpec(memory_space=pl.ANY)
VM = pl.BlockSpec(memory_space=pltpu.VMEM)


def call(kernel, ins, outs, scratch=(), limit=VMEM_LIMIT, flops=None, aliases=None):
    cost = None if flops is None else pl.CostEstimate(flops=flops, bytes_accessed=1_000_000, transcendentals=0)
    return pl.pallas_call(
        kernel,
        out_shape=outs,
        in_specs=ins,
        scratch_shapes=list(scratch),
        cost_estimate=cost,
        input_output_aliases=aliases or {},
        compiler_params=pltpu.CompilerParams(vmem_limit_bytes=limit),
    )


def struct(shape, kind):
    return jax.ShapeDtypeStruct(shape, kind)


def buffer(*shape):
    return pltpu.VMEM(shape, F32)


def buffer16(*shape):
    return pltpu.VMEM(shape, BF16)


def shift(value, axes, step):
    n = lax.axis_size(axes)
    return lax.ppermute(value, axes, [(i, (i + step) % n) for i in range(n)])


def partner(value, axes, bits):
    n = lax.axis_size(axes)
    return lax.ppermute(value, axes, [(i, i ^ bits) for i in range(n)])


TX = ("x", "yh")
TY = ("z", "core")


def on_device(density, kernel_one, kernel_two, cotangent):
    d, c = density[0], cotangent[0]
    k1 = jnp.transpose(kernel_one, (2, 3, 4, 1, 0)).reshape(27, CIN, CH)
    k2 = jnp.transpose(kernel_two, (2, 3, 4, 0, 1)).reshape(27, CH, CH)

    message = struct((128, 128), BF16)
    yup, ydown = call(
        pack_y_kernel,
        [ANY] * 2,
        (message, message),
        (
            buffer16(2, NXT, 16, 128), buffer16(2, HX, 16, 256),
            buffer(NXT * 16, 128), buffer(2, HX * 16, 128), pltpu.SemaphoreType.DMA((4,)),
        ),
        limit=VMEM_SPARE,
        flops=FLOPS,
    )(d, c)
    lo, hi = shift(yup, TY, 1), shift(ydown, TY, -1)
    w1, wb = call(
        weights_kernel,
        [VM] * 2,
        (struct((2, 256, 768), BF16), struct((256, 2304), BF16)),
        (buffer(128, 128), buffer(16, 19 * 128), buffer(64, 2048)),
    )(k1, k2)
    fine = struct((NXT * HY, 512), BF16)
    taps = call(
        tap_kernel,
        [VM] * 2,
        (fine, fine, struct((NXT * HY, 256), BF16), struct((HX * HY, 768), BF16)),
        (buffer(NXT * DROW, 128), buffer(NXT * DROW, 128), buffer(2, HX * CROW, 128)),
    )(d, c)
    message = struct((288, 128), BF16)
    up, down = call(
        pack_x_kernel,
        [VM] * 4 + [ANY] * 2,
        (message, message),
        (buffer(128, 128), buffer(128, 128), buffer(32, 128)),
    )(d, c, lo, hi, w1, taps[3])
    xlo, xhi = shift(up, TX, 1), shift(down, TX, -1)

    *taps, pool, g1 = call(
        inner_kernel,
        [VM] * 8,
        tuple(struct(tap.shape, BF16) for tap in taps) + (struct((256, 384), BF16), struct((2, 256, 768), F32)),
        (buffer(128, 128), buffer(128, 128), buffer(2, 32, 512), buffer16(2, 1536, 768), buffer16(2, 256, 1536)),
        aliases={0: 0, 1: 1, 2: 2, 3: 3},
    )(*taps, lo, hi, w1, wb)
    gradient = struct((24, 512), BF16)
    rim = struct((6 * HY, 512), BF16)
    grads, outer, *rims = call(
        edge_kernel,
        [VM] * 10,
        (gradient, struct((256, 128), BF16), rim, rim, struct((6 * HY, 256), BF16)),
        (
            buffer(6 * DROW, 128), buffer(6 * DROW, 128), buffer(2, 2 * CROW, 128), buffer(64, 128), buffer(2, 32, 128),
            buffer16(2 * HY, 768), buffer16(2, 512, 768),
            buffer(2, 256, 768), buffer(256, 2304), buffer(512, 128), buffer(512, 256),
        ),
    )(*taps, xlo, xhi, w1, wb, pool, g1)

    grads = call(add_two_kernel, [VM] * 2, gradient)(grads, partner(grads, "core", 1))
    w2 = call(
        feature_weights_kernel,
        [VM, ANY],
        struct((256, 2304), BF16),
        (buffer(64, 128), buffer(64, 2048)),
    )(k2, grads)
    edge = call(
        rim_kernel,
        [ANY] + [VM] * 13,
        struct((128, 256), BF16),
        (
            buffer(2, 8, 48, 128), buffer(8, 48, 128), buffer(288, 128), buffer(2, 2, 48, 128), buffer16(2, 512, 768),
        ),
    )(grads, yup, ydown, lo, hi, xlo, xhi, *taps[:3], *rims, w1)
    others = [partner(grads, "z", bits) for bits in (1, 3, 2)]
    grads = call(add_four_kernel, [VM] * 4 + [ANY] * 2, gradient)(grads, *others, edge, w2)
    feat, token = call(
        feature_kernel,
        [ANY] + [VM] * 4,
        (struct((HX, HY, 256), BF16), struct((8, 128), F32)),
        (buffer(2, (HX + 2) * CROW, 128), buffer16((HX + 2) * HY, 768)),
    )(grads, edge, pool, outer, w2)
    others = [partner(grads, "x", bits) for bits in (1, 3, 2)]
    grads = call(add_four_kernel, [VM] * 4 + [ANY] * 2, gradient)(grads, *others, token, token)
    near = partner(grads, "rep", 1)
    across = partner(grads, ("rep", "yh"), 3)
    far = partner(grads, "yh", 1)
    g1, g2 = call(final_kernel, [VM] * 4, (struct((27, CIN, CH), F32), struct((27, CH, CH), F32)))(
        grads, near, across, far
    )
    g1 = jnp.transpose(g1.reshape(3, 3, 3, CIN, CH), (4, 3, 0, 1, 2))
    g2 = jnp.transpose(g2.reshape(3, 3, 3, CH, CH), (3, 4, 0, 1, 2))
    return feat[None], g1, g2


def solution(mesh):
    fine = Mesh(mesh.devices.reshape(2, 4, 2, 4, 2), ("rep", "x", "yh", "z", "core"))
    tiles = P("rep", TX, TY, None)
    return jax.shard_map(
        on_device, mesh=fine, in_specs=(tiles, P(), P(), tiles), out_specs=(tiles, P(), P()), check_vma=False
    )
```

```python
import jax
import jax.numpy as jnp
from jax import lax
from jax.experimental import pallas as pl
from jax.experimental.pallas import tpu as pltpu
from jax.sharding import Mesh
from jax.sharding import PartitionSpec as P

CIN = 4
CH = 16
LEAK = 0.3
F32 = jnp.float32
BF16 = jnp.bfloat16
NXT = 32
NYT = 64
HX = NXT // 2
HY = NYT // 2
DROW = 80
CROW = 48
BULK = tuple(range(2, HX - 2))
INNER = BULK + (1, HX - 2)
OUTER = (0, HX - 1)
VMEM_LIMIT = 32 * 1024 * 1024
FLOPS = 5_000_000_000
VMEM_SPARE = 55050 * 1024


def dot_nt(lhs, rhs):
    return lax.dot_general(lhs, rhs, (((1,), (1,)), ((), ())), preferred_element_type=F32)


def dot_nn(lhs, rhs):
    return lax.dot_general(lhs, rhs, (((1,), (0,)), ((), ())), preferred_element_type=F32)


def iota(shape, dim):
    return lax.broadcasted_iota(jnp.int32, shape, dim)


def pack_y_kernel(d_hbm, c_hbm, up_ref, down_ref, db, cb, ds, cs, sem):
    copies = []
    for low in range(2):
        at, cat = (NYT - 16, HY - 16) if low == 0 else (0, 0)
        copies.append(pltpu.make_async_copy(d_hbm.at[:, pl.ds(at, 16), :], db.at[low], sem.at[2 * low]))
        copies.append(pltpu.make_async_copy(c_hbm.at[:, pl.ds(cat, 16), :], cb.at[low], sem.at[2 * low + 1]))
    for copy in copies:
        copy.start()
    for copy in copies:
        copy.wait()
    for low, out, row, crow in ((0, up_ref, 13, 15), (1, down_ref, 0, 0)):
        ds[...] = db[low].astype(F32).reshape(NXT * 16, 128)
        for half in range(2):
            cs[half] = cb[low, :, :, half * 128 : half * 128 + 128].astype(F32).reshape(HX * 16, 128)
        for k in range(3):
            out[k * 32 : k * 32 + 32, :] = ds[pl.ds(row + k, 32, stride=16), :].astype(BF16)
        for half in range(2):
            edge = cs[half, pl.ds(crow, 16, stride=16), :]
            out[96 + half * 16 : 112 + half * 16, :] = edge.astype(BF16)


def pack_x_kernel(d_ref, c_ref, lo_ref, hi_ref, after_ref, also_ref, up_ref, down_ref, ls, hs, ms):
    ls[...] = lo_ref[...].astype(F32)
    hs[...] = hi_ref[...].astype(F32)
    for out, x, cx in ((down_ref, 0, 0), (up_ref, NXT - 3, HX - 1)):
        out[0:192, :] = d_ref[x : x + 3, :, :].reshape(192, 128)
        out[192:224, :] = c_ref[cx, :, 0:128]
        out[224:256, :] = c_ref[cx, :, 128:256]
        for side, src in enumerate((ls, hs)):
            for k in range(3):
                ms[side * 9 + 3 * k : side * 9 + 3 * k + 3, :] = src[k * 32 + x : k * 32 + x + 3, :]
            for half in range(2):
                at = 18 + side * 2 + half
                ms[at : at + 1, :] = src[96 + half * 16 + cx : 97 + half * 16 + cx, :]
        ms[22:32, :] = jnp.zeros((10, 128), F32)
        out[256:288, :] = ms[...].astype(BF16)


def weights_kernel(k1_ref, k2_ref, w1_ref, wb_ref, s1, c1, cb):
    for t in range(27):
        s1[4 * t : 4 * t + 4, 0:CH] = k1_ref[t].astype(F32)
    s1[108:128, :] = jnp.zeros((20, 128), F32)
    k1t = s1[...].T[0:CH].astype(BF16)
    t27, i = iota((128, 128), 0) // 4, iota((128, 128), 0) % 4
    lane = iota((128, 128), 1)
    spread = []
    for kd in range(3):
        for b in range(5):
            tap = 2 * b + lane // 64
            spread.append((t27 == kd * 9 + tap) & (tap <= 8) & (i == lane % 64 // 16))
    u = lane - 64
    for h in range(2):
        for py in range(2):
            kx, ky = u // 16, u % 16 // 4 - py
            good = (u >= 0) & (kx <= 2) & (ky >= 0) & (ky <= 2) & (i == u % 4)
            spread.append((t27 == (2 - 2 * h) * 9 + kx * 3 + ky) & good)
    c1[...] = dot_nn(k1t, jnp.concatenate([part.astype(BF16) for part in spread], axis=1))
    groups = []
    for g in range(4):
        for j in range(8):
            if g * 8 + j < 27:
                s1[j * 16 : j * 16 + 16, 0:CH] = k2_ref[g * 8 + j].astype(F32)
        groups.append(s1[...].T[0:CH])
    rep2 = (iota((128, 2048), 0) == iota((128, 2048), 1) // 16).astype(BF16)
    cb[...] = dot_nn(jnp.concatenate(groups, axis=0).astype(BF16), rep2)

    depth1 = iota((16, 128), 1) % 16
    depth2 = iota((16, 256), 1) % 16
    for h in range(2):
        for n in range(16):
            row = (n % 2) * 128 + (n // 2) * 16
            touches = n == 15 - 15 * h
            for b in range(6):
                acc = jnp.zeros((16, 128), F32)
                if b < 5:
                    for kd in range(3):
                        at = (kd * 5 + b) * 128
                        acc = jnp.where(depth1 == n + kd - 1, c1[:, at : at + 128], acc)
                if b >= 4 and touches:
                    at = (15 + 2 * h + b - 4) * 128
                    acc = acc + c1[:, at : at + 128]
                w1_ref[h, row : row + 16, b * 128 : b * 128 + 128] = acc.astype(BF16)
    for kx in range(3):
        for ky in range(3):
            ts = [kd * 9 + kx * 3 + ky for kd in range(3)]
            at = ((2 - kx) * 3 + 2 - ky) * 256
            backs = [cb[t // 8 * 16 : t // 8 * 16 + 16, t % 8 * 256 : t % 8 * 256 + 256] for t in ts]
            for d in range(16):
                acc = jnp.zeros((16, 256), F32)
                for kd in range(3):
                    acc = jnp.where(depth2 == d + 1 - kd, backs[kd], acc)
                wb_ref[d * 16 : d * 16 + 16, at : at + 256] = acc.astype(BF16)


def feature_weights_kernel(k2_ref, after_ref, w2_ref, so, cf):
    so[...] = jnp.zeros(so.shape, F32)
    for t in range(27):
        g, j = t // 8, t % 8
        so[g * 16 : g * 16 + 16, j * 16 : j * 16 + 16] = k2_ref[t].astype(F32)
    row, lane = iota((128, 2048), 0), iota((128, 2048), 1)
    rep2 = ((row // 16 == lane // 256) & (row % 16 == lane % 16)).astype(BF16)
    cf[...] = dot_nn(so[...].astype(BF16), rep2)
    gap = iota((1, 16, 256), 2) // 16 - iota((1, 16, 256), 1)
    for m in range(9):
        acc = jnp.zeros((16, 16, 256), F32)
        for kd in range(3):
            t = kd * 9 + m
            part = cf[t // 8 * 16 : t // 8 * 16 + 16, t % 8 * 256 : t % 8 * 256 + 256]
            acc = jnp.where(gap == kd - 1, part[:, None, :], acc)
        w2_ref[:, m * 256 : m * 256 + 256] = acc.reshape(256, 256).astype(BF16)


def halves_matrix():
    row, col = iota((128, 256), 0), iota((128, 256), 1)
    place = row % 32 // 16 * 64 + row // 32 * 16 + row % 16
    return (place == (col + col // 128 * 64) % 128).astype(BF16)


def touch_matrix():
    row, col = iota((512, 256), 0), iota((512, 256), 1)
    u = col % 128 - 64
    lane = jnp.where(col < 128, 64 + u % 4 * 16, u % 4 * 16 + 15)
    return ((row // 128 == u % 16 // 4) & (row % 128 == lane) & (u >= 0)).astype(BF16)


def fine_taps(dp, ds, ft, fs, vt, layers):
    for n in range(layers):
        for t in range(4):
            for src, out in ((dp, ft), (ds, fs)):
                rows = src[pl.ds(n * DROW + 7 + t, HY, stride=2), :]
                out[n * HY : n * HY + HY, t * 128 : t * 128 + 128] = rows.astype(BF16)
    vt[...] = dot_nn(ft[...], touch_matrix()).astype(BF16)


def coarse_taps(padded, taps, layers):
    for n in range(layers):
        for k in range(3):
            for half in range(2):
                rows = padded[half, n * CROW + 7 + k : n * CROW + 7 + k + HY, :]
                lane = k * 256 + half * 128
                taps[n * HY : n * HY + HY, lane : lane + 128] = rows.astype(BF16)


def pick(low, first, second):
    return jnp.where(low, first, second)


def patch_blocks(h, py, plain, swapped, touch, rows):
    lane = iota((rows, 128), 1)
    low = lane < 64
    first, second = (plain, swapped) if h == 0 else (swapped, plain)
    blocks = [pick(low, first(2 * b // 3, 2 * b % 3), second((2 * b + 1) // 3, (2 * b + 1) % 3)) for b in range(4)]
    zero = jnp.zeros((rows, 128), BF16)
    edge = pick(lane < 80, touch(0), pick(lane < 96, touch(1), touch(2)))
    blocks.append(pick(low, first(2, 2), edge if py == 0 else zero))
    blocks.append(edge if py == 1 else zero)
    return blocks


def cell_patch(h, fine, rims, cell, px, py):
    def layer(which, x, lanes):
        if 0 <= x < NXT:
            return fine[which][x * HY : x * HY + HY, lanes]
        n = x + 3 if x < 0 else x - NXT + 3
        return rims[which][n * HY : n * HY + HY, lanes]

    def tap(which):
        return lambda kx, ky: layer(which, 2 * cell + px + kx - 1, slice((py + ky) * 128, (py + ky) * 128 + 128))

    def touch(kx):
        return layer(2, 2 * cell + px + kx - 1, slice(h * 128, h * 128 + 128))

    return jnp.concatenate(patch_blocks(h, py, tap(0), tap(1), touch, HY), axis=1)


def group_patch(h, fine, rims, cells):
    rows = [cell_patch(h, fine, rims, cell, c // 2, c % 2) for c in range(4) for cell in cells]
    return jnp.concatenate(rows, axis=0)


def store_patch(out, h, at, fine, rims, cell, px, py):
    out[h, at : at + HY, :] = cell_patch(h, fine, rims, cell, px, py)


def coarse_patch(taps, rims, cells):
    rows = []
    for cell in cells:
        parts = []
        for x in (cell - 1, cell, cell + 1):
            ref, n = (taps, x) if 0 <= x < HX else (rims, 0 if x < 0 else 1)
            parts.append(ref[n * HY : n * HY + HY, :])
        rows.append(jnp.concatenate(parts, axis=1))
    return jnp.concatenate(rows, axis=0)


def pooled_sum(pres):
    parts = []
    for pre in pres:
        total = jnp.zeros((128, 128), F32)
        for at in range(0, pre.shape[1], 128):
            part = pre[:, at : at + 128]
            act = jnp.where(part > 0, part, LEAK * part).astype(BF16).astype(F32)
            total = total + act[0:128] + act[128:256]
        if pre.shape[1] == 256:
            total = total + pltpu.roll(total, 64, axis=1)
        parts.append(total * 0.125)
    return jnp.concatenate(parts, axis=0)


def back_through(h, pre, back):
    part = back[h * 128 : h * 128 + 128]
    both = jnp.concatenate([part, part], axis=0)
    low = LEAK * both
    return [jnp.where(pre[:, at : at + 128] > 0, both, low).astype(BF16) for at in range(0, pre.shape[1], 128)]


def tap_kernel(d_ref, c_ref, ft_ref, fs_ref, vt_ref, ct_ref, dp, ds, cp):
    both = dot_nn(d_ref[...].reshape(NXT * NYT, 128), halves_matrix())
    for n, out in enumerate((dp, ds)):
        for x in range(NXT):
            out[x * DROW + 8 : x * DROW + 8 + NYT, :] = both[x * NYT : x * NYT + NYT, n * 128 : n * 128 + 128]
        for y in (7, 8 + NYT):
            out[pl.ds(y, NXT, stride=DROW), :] = jnp.zeros((NXT, 128), F32)
    for half in range(2):
        for x in range(HX):
            at = x * CROW + 8
            cp[half, at : at + HY, :] = c_ref[x, :, half * 128 : half * 128 + 128].astype(F32)
    fine_taps(dp, ds, ft_ref, fs_ref, vt_ref, NXT)
    coarse_taps(cp, ct_ref, HX)


def set_row(ref, block, lanes, row, value, tap=None):
    old = ref[block : block + 16, lanes].astype(F32)
    where = iota(old.shape, 0) == row
    if tap is not None:
        where = where & (iota(old.shape, 1) % 16 // 4 == tap)
    ref[block : block + 16, lanes] = jnp.where(where, value, old).astype(BF16)


def inner_kernel(
    ft_in, fs_in, vt_in, ct_in, lo_ref, hi_ref, w1_ref, wb_ref, ft, fs, vt, ct, pool_ref, g1_ref, ls, hs, ys, pa, bpre
):
    ls[...] = lo_ref[...].astype(F32)
    hs[...] = hi_ref[...].astype(F32)
    touch = touch_matrix()
    for n, rows, t in ((0, lo_ref[64:96, :], 0), (1, hi_ref[0:32, :], 3)):
        both = dot_nn(rows, halves_matrix())
        ys[n, :, 0:256] = both
        ys[n, :, 256:512] = dot_nn(both[:, 0:128].astype(BF16), touch[t * 128 : t * 128 + 128])
    for x in range(NXT):
        for n, block, row, t in ((0, x * HY, 0, 0), (1, x * HY + 16, 15, 3)):
            lanes = slice(t * 128, t * 128 + 128)
            set_row(ft, block, lanes, row, ys[n, x : x + 1, 0:128])
            set_row(fs, block, lanes, row, ys[n, x : x + 1, 128:256])
            set_row(vt, block, slice(0, 256), row, ys[n, x : x + 1, 256:512], t)
    for x in range(HX):
        for half in range(2):
            at = 96 + half * 16 + x
            set_row(ct, x * HY, slice(half * 128, half * 128 + 128), 0, ls[at : at + 1, :])
            set_row(ct, x * HY + 16, slice(512 + half * 128, 640 + half * 128), 15, hs[at : at + 1, :])
    back = dot_nt(wb_ref[...], coarse_patch(ct, None, INNER + INNER[12:])).astype(BF16).astype(F32) * 0.125
    for g in range(4):
        cells = INNER[4 * g : 4 * g + 4]
        size = len(cells) * 128
        pres = []
        for h in range(2):
            patch = group_patch(h, (ft, fs, vt), None, cells)
            pa[h, g * 512 : g * 512 + size, :] = patch
            pres.append(dot_nt(w1_ref[h], patch))
        pool_ref[:, g * 128 : g * 128 + 128] = pooled_sum(pres).astype(BF16)
        for h in range(2):
            part = jnp.concatenate(back_through(h, pres[h], back[:, g * 128 : g * 128 + 128]), axis=1)
            bpre[h, :, g * 512 : g * 512 + size] = part
    for h in range(2):
        g1_ref[h] = dot_nn(bpre[h], pa[h])


def split_dot(select, values):
    high = values.astype(BF16)
    low = (values - high.astype(F32)).astype(BF16)
    return dot_nt(select, high) + dot_nt(select, low)


def extract(g1, g2, out_ref, a1, a2):
    depth1 = iota((16, 128), 1) % 16
    depth2 = iota((16, 256), 1) % 16
    row, col = iota((256, 640), 0), iota((256, 640), 1)
    u = row % 128 - 64
    tap = u // 16 * 3 + u % 16 // 4 - row // 128
    ky = u % 16 // 4 - row // 128
    good = (u >= 0) & (u < 48) & (ky >= 0) & (ky <= 2)
    place = (good & (col == tap // 2 * 128 + tap % 2 * 64 + u % 4 * 16)).astype(BF16)
    touch = jnp.concatenate([g1[0, 240:256, 512:768], g1[1, 0:16, 512:768]], axis=0)
    high = touch.astype(BF16)
    touch = dot_nn(high, place) + dot_nn((touch - high.astype(F32)).astype(BF16), place)
    for b in range(5):
        lanes = slice(b * 128, b * 128 + 128)
        total = [touch[16:32, lanes], jnp.zeros((16, 128), F32), touch[0:16, lanes]]
        for h in range(2):
            acc = [jnp.zeros((16, 128), F32)] * 3
            for n in range(16):
                row = (n % 2) * 128 + (n // 2) * 16
                part = g1[h, row : row + 16, lanes]
                acc = [jnp.where(depth1 == n + kd - 1, part, acc[kd]) for kd in range(3)]
            total = [total[kd] + acc[kd] for kd in range(3)]
        for kd in range(3):
            a1[(b * 3 + kd) * 16 : (b * 3 + kd) * 16 + 16, :] = total[kd]
    for m in range(9):
        acc = [jnp.zeros((16, 256), F32)] * 3
        for d in range(16):
            part = g2[d * 16 : d * 16 + 16, m * 256 : m * 256 + 256]
            acc = [jnp.where(depth2 == d + 1 - kd, part, acc[kd]) for kd in range(3)]
        for kd in range(3):
            a2[(m * 3 + kd) * 16 : (m * 3 + kd) * 16 + 16, :] = acc[kd]
    a1[240:256, :] = jnp.zeros((16, 128), F32)
    a2[432:512, :] = jnp.zeros((80, 256), F32)
    pick2 = (iota((16, 256), 1) // 16 == iota((16, 256), 0)).astype(BF16)
    pick1 = (iota((16, 128), 1) // 16 == iota((16, 128), 0)).astype(BF16)
    two = split_dot(pick2, a2[...])
    one = jnp.concatenate([split_dot(pick1, a1[...])[0:8], jnp.zeros((8, 256), F32)], axis=1)
    out_ref[...] = jnp.concatenate([two, one], axis=0).astype(BF16)


def edge_kernel(
    ft, fs, vt, ct, xlo_ref, xhi_ref, w1_ref, wb_ref, pool_ref, g1_ref,
    grad_ref, all_ref, rft, rfs, rvt, dp, ds, cp, corner, swapped, crims, pa, g1, g2, a1, a2,
):
    for zone, src in enumerate((xlo_ref, xhi_ref)):
        both = dot_nn(jnp.concatenate([src[0:192, :], src[256:288, :]], axis=0), halves_matrix())
        for k in range(3):
            at = (zone * 3 + k) * DROW + 8
            dp[at : at + NYT, :] = both[k * 64 : k * 64 + 64, 0:128]
            ds[at : at + NYT, :] = both[k * 64 : k * 64 + 64, 128:256]
        swapped[0] = both[192:224, 0:128]
        swapped[1] = both[192:224, 128:256]
        corner[zone * 32 : zone * 32 + 32, :] = src[256:288, :].astype(F32)
        for side, y in ((0, 5), (1, 8 + NYT)):
            for ky in range(3):
                for kx in range(3):
                    row = (zone * 3 + kx) * DROW + y + ky
                    at = side * 9 + 3 * ky + kx
                    dp[row : row + 1, :] = swapped[0, at : at + 1, :]
                    ds[row : row + 1, :] = swapped[1, at : at + 1, :]
        for half in range(2):
            at = zone * CROW + 8
            cp[half, at : at + HY, :] = src[192 + half * 32 : 224 + half * 32, :].astype(F32)
            for side, y in ((0, 7), (1, 8 + HY)):
                at = zone * 32 + 18 + side * 2 + half
                cp[half, zone * CROW + y : zone * CROW + y + 1, :] = corner[at : at + 1, :]
    fine_taps(dp, ds, rft, rfs, rvt, 6)
    coarse_taps(cp, crims, 2)
    cpatch = coarse_patch(ct, crims, OUTER)
    back = dot_nt(wb_ref[...], jnp.concatenate([cpatch, cpatch], axis=0)).astype(BF16).astype(F32) * 0.125
    pres = []
    for h in range(2):
        patch = group_patch(h, (ft, fs, vt), (rft, rfs, rvt), OUTER)
        pa[h] = patch
        pres.append(dot_nt(w1_ref[h], patch))
    mean = pooled_sum(pres).astype(BF16)
    last = jnp.where(iota((256, 128), 1) < 64, pool_ref[:, 384:512], mean)
    pooled = jnp.concatenate([pool_ref[:, 0:384], last], axis=1)
    all_ref[...] = pooled
    for h in range(2):
        g1[h] = g1_ref[h] + dot_nn(jnp.concatenate(back_through(h, pres[h], back), axis=1), pa[h])
    g2[...] = dot_nn(pooled, jnp.concatenate([coarse_patch(ct, None, INNER), cpatch], axis=0))
    extract(g1, g2, grad_ref, a1, a2)


def rim_kernel(
    after_ref, up_ref, down_ref, lo_ref, hi_ref, xlo_ref, xhi_ref, ft, fs, vt, rft, rfs, rvt, w1_ref,
    edge_ref, col, raw, corner, tv, rim,
):
    raw[...] = jnp.zeros(raw.shape, F32)
    for k in range(3):
        raw[k, 8:40, :] = lo_ref[k * 32 : k * 32 + 32, :].astype(F32)
        raw[5 + k, 8:40, :] = hi_ref[k * 32 : k * 32 + 32, :].astype(F32)
    raw[3, 8:40, :] = down_ref[0:32, :].astype(F32)
    raw[4, 8:40, :] = up_ref[64:96, :].astype(F32)
    for src, row in ((xlo_ref, 5), (xhi_ref, 40)):
        corner[...] = src[...].astype(F32)
        for kx in range(3):
            for ky in range(3):
                raw[ky, row + kx : row + kx + 1, :] = corner[256 + 3 * ky + kx : 257 + 3 * ky + kx, :]
                raw[5 + ky, row + kx : row + kx + 1, :] = corner[265 + 3 * ky + kx : 266 + 3 * ky + kx, :]
            raw[3, row + kx : row + kx + 1, :] = corner[kx * 64 : kx * 64 + 1, :]
            raw[4, row + kx : row + kx + 1, :] = corner[kx * 64 + 63 : kx * 64 + 64, :]
    both = dot_nn(raw[...].reshape(8 * 48, 128).astype(BF16), halves_matrix())
    touch = touch_matrix()
    for side in range(2):
        parts = []
        for t in range(4):
            part = both[(side * 4 + t) * 48 : (side * 4 + t) * 48 + 48]
            col[0, side * 4 + t] = part[:, 0:128]
            col[1, side * 4 + t] = part[:, 128:256]
            parts.append(part[:, 0:128].astype(BF16))
        ends = dot_nn(jnp.concatenate(parts, axis=1), touch)
        tv[side, 0] = ends[:, 0:128]
        tv[side, 1] = ends[:, 128:256]
    blank = jnp.zeros((14, 128), F32)
    for h in range(2):
        for px in range(2):
            for py in range(2):
                at = (px * 2 + py) * 128
                for n, cell in enumerate((-1, HX)):
                    store_patch(rim, h, at + n * HY, (ft, fs, vt), (rft, rfs, rvt), cell, px, py)
                for side in range(2):

                    def tap(which):
                        def get(kx, ky):
                            rows = col[which, side * 4 + py + ky, pl.ds(5 + px + kx, 18, stride=2), :]
                            return jnp.concatenate([rows, blank], axis=0).astype(BF16)

                        return get

                    def ends_of(kx):
                        rows = tv[side, h, pl.ds(5 + px + kx, 18, stride=2), :]
                        return jnp.concatenate([rows, blank], axis=0).astype(BF16)

                    top = at + 64 + side * 32
                    for b, block in enumerate(patch_blocks(h, py, tap(0), tap(1), ends_of, 32)):
                        rim[h, top : top + 32, b * 128 : b * 128 + 128] = block
    pres = [dot_nt(w1_ref[h], rim[h]) for h in range(2)]
    edge_ref[...] = pooled_sum(pres).T.astype(BF16)


def feature_kernel(after_ref, edge_ref, pool_ref, w2_ref, feat_ref, token_ref, pp, pt):
    edge = edge_ref[...].astype(F32)
    inner = pool_ref[...].astype(F32).T
    for half in range(2):
        lanes = slice(half * 128, half * 128 + 128)
        pp[half, 8:40, :] = edge[0:32, lanes]
        pp[half, (HX + 1) * CROW + 8 : (HX + 1) * CROW + 40, :] = edge[32:64, lanes]
        for n, x in enumerate(INNER + OUTER):
            pp[half, (x + 1) * CROW + 8 : (x + 1) * CROW + 40, :] = inner[n * 32 : n * 32 + 32, lanes]
        pp[half, pl.ds(7, 18, stride=CROW), :] = edge[64:82, lanes]
        pp[half, pl.ds(8 + HY, 18, stride=CROW), :] = edge[96:114, lanes]
    coarse_taps(pp, pt, HX + 2)
    patch = [pt[k * HY : (k + HX) * HY, :] for k in range(3)]
    feat = dot_nt(jnp.concatenate(patch, axis=1), w2_ref[...])
    feat_ref[...] = feat.astype(BF16).reshape(HX, HY, 256)
    token_ref[...] = feat[0:8, 0:128]


def add_two_kernel(a_ref, b_ref, out_ref):
    out_ref[...] = (a_ref[...].astype(F32) + b_ref[...].astype(F32)).astype(BF16)


def add_four(refs):
    a, b, c, d = (ref[...].astype(F32) for ref in refs)
    return (a + b) + (c + d)


def add_four_kernel(a_ref, b_ref, c_ref, d_ref, after_ref, also_ref, out_ref):
    out_ref[...] = add_four((a_ref, b_ref, c_ref, d_ref)).astype(BF16)


def final_kernel(a_ref, b_ref, c_ref, d_ref, g1_ref, g2_ref):
    total = add_four((a_ref, b_ref, c_ref, d_ref)) * 0.5
    for kd in range(3):
        for kx in range(3):
            for ky in range(3):
                t, m = kd * 9 + kx * 3 + ky, kx * 3 + ky
                at, row = (m // 2 * 3 + kd) * 16, 16 + m % 2 * 4
                g1_ref[t] = total[row : row + 4, at : at + 16]
                at = (((2 - kx) * 3 + 2 - ky) * 3 + kd) * 16
                g2_ref[t] = total[0:16, at : at + 16]


ANY = pl.BlockSpec(memory_space=pl.ANY)
VM = pl.BlockSpec(memory_space=pltpu.VMEM)


def call(kernel, ins, outs, scratch=(), limit=VMEM_LIMIT, flops=None, aliases=None):
    cost = None if flops is None else pl.CostEstimate(flops=flops, bytes_accessed=1_000_000, transcendentals=0)
    return pl.pallas_call(
        kernel,
        out_shape=outs,
        in_specs=ins,
        scratch_shapes=list(scratch),
        cost_estimate=cost,
        input_output_aliases=aliases or {},
        compiler_params=pltpu.CompilerParams(vmem_limit_bytes=limit),
    )


def struct(shape, kind):
    return jax.ShapeDtypeStruct(shape, kind)


def buffer(*shape):
    return pltpu.VMEM(shape, F32)


def buffer16(*shape):
    return pltpu.VMEM(shape, BF16)


def shift(value, axes, step):
    n = lax.axis_size(axes)
    return lax.ppermute(value, axes, [(i, (i + step) % n) for i in range(n)])


def partner(value, axes, bits):
    n = lax.axis_size(axes)
    return lax.ppermute(value, axes, [(i, i ^ bits) for i in range(n)])


TX = ("x", "yh")
TY = ("z", "core")


def on_device(density, kernel_one, kernel_two, cotangent):
    d, c = density[0], cotangent[0]
    k1 = jnp.transpose(kernel_one, (2, 3, 4, 1, 0)).reshape(27, CIN, CH)
    k2 = jnp.transpose(kernel_two, (2, 3, 4, 0, 1)).reshape(27, CH, CH)

    message = struct((128, 128), BF16)
    yup, ydown = call(
        pack_y_kernel,
        [ANY] * 2,
        (message, message),
        (
            buffer16(2, NXT, 16, 128), buffer16(2, HX, 16, 256),
            buffer(NXT * 16, 128), buffer(2, HX * 16, 128), pltpu.SemaphoreType.DMA((4,)),
        ),
        limit=VMEM_SPARE,
        flops=FLOPS,
    )(d, c)
    lo, hi = shift(yup, TY, 1), shift(ydown, TY, -1)
    w1, wb = call(
        weights_kernel,
        [VM] * 2,
        (struct((2, 256, 768), BF16), struct((256, 2304), BF16)),
        (buffer(128, 128), buffer(16, 19 * 128), buffer(64, 2048)),
    )(k1, k2)
    fine = struct((NXT * HY, 512), BF16)
    taps = call(
        tap_kernel,
        [VM] * 2,
        (fine, fine, struct((NXT * HY, 256), BF16), struct((HX * HY, 768), BF16)),
        (buffer(NXT * DROW, 128), buffer(NXT * DROW, 128), buffer(2, HX * CROW, 128)),
    )(d, c)
    message = struct((288, 128), BF16)
    up, down = call(
        pack_x_kernel,
        [VM] * 4 + [ANY] * 2,
        (message, message),
        (buffer(128, 128), buffer(128, 128), buffer(32, 128)),
    )(d, c, lo, hi, w1, taps[3])
    xlo, xhi = shift(up, TX, 1), shift(down, TX, -1)

    *taps, pool, g1 = call(
        inner_kernel,
        [VM] * 8,
        tuple(struct(tap.shape, BF16) for tap in taps) + (struct((256, 512), BF16), struct((2, 256, 768), F32)),
        (buffer(128, 128), buffer(128, 128), buffer(2, 32, 512), buffer16(2, 1792, 768), buffer16(2, 256, 1792)),
        aliases={0: 0, 1: 1, 2: 2, 3: 3},
    )(*taps, lo, hi, w1, wb)
    gradient = struct((24, 512), BF16)
    rim = struct((6 * HY, 512), BF16)
    grads, pool, *rims = call(
        edge_kernel,
        [VM] * 10,
        (gradient, struct((256, 512), BF16), rim, rim, struct((6 * HY, 256), BF16)),
        (
            buffer(6 * DROW, 128), buffer(6 * DROW, 128), buffer(2, 2 * CROW, 128), buffer(64, 128), buffer(2, 32, 128),
            buffer16(2 * HY, 768), buffer16(2, 256, 768),
            buffer(2, 256, 768), buffer(256, 2304), buffer(256, 128), buffer(512, 256),
        ),
    )(*taps, xlo, xhi, w1, wb, pool, g1)

    grads = call(add_two_kernel, [VM] * 2, gradient)(grads, partner(grads, "core", 1))
    w2 = call(
        feature_weights_kernel,
        [VM, ANY],
        struct((256, 2304), BF16),
        (buffer(64, 128), buffer(64, 2048)),
    )(k2, grads)
    edge = call(
        rim_kernel,
        [ANY] + [VM] * 13,
        struct((128, 256), BF16),
        (
            buffer(2, 8, 48, 128), buffer(8, 48, 128), buffer(288, 128), buffer(2, 2, 48, 128), buffer16(2, 512, 768),
        ),
    )(grads, yup, ydown, lo, hi, xlo, xhi, *taps[:3], *rims, w1)
    others = [partner(grads, "z", bits) for bits in (1, 3, 2)]
    grads = call(add_four_kernel, [VM] * 4 + [ANY] * 2, gradient)(grads, *others, edge, w2)
    feat, token = call(
        feature_kernel,
        [ANY] + [VM] * 3,
        (struct((HX, HY, 256), BF16), struct((8, 128), F32)),
        (buffer(2, (HX + 2) * CROW, 128), buffer16((HX + 2) * HY, 768)),
    )(grads, edge, pool, w2)
    others = [partner(grads, "x", bits) for bits in (1, 3, 2)]
    grads = call(add_four_kernel, [VM] * 4 + [ANY] * 2, gradient)(grads, *others, token, token)
    near = partner(grads, "rep", 1)
    across = partner(grads, ("rep", "yh"), 3)
    far = partner(grads, "yh", 1)
    g1, g2 = call(final_kernel, [VM] * 4, (struct((27, CIN, CH), F32), struct((27, CH, CH), F32)))(
        grads, near, across, far
    )
    g1 = jnp.transpose(g1.reshape(3, 3, 3, CIN, CH), (4, 3, 0, 1, 2))
    g2 = jnp.transpose(g2.reshape(3, 3, 3, CH, CH), (3, 4, 0, 1, 2))
    return feat[None], g1, g2


def solution(mesh):
    fine = Mesh(mesh.devices.reshape(2, 4, 2, 4, 2), ("rep", "x", "yh", "z", "core"))
    tiles = P("rep", TX, TY, None)
    return jax.shard_map(
        on_device, mesh=fine, in_specs=(tiles, P(), P(), tiles), out_specs=(tiles, P(), P()), check_vma=False
    )
```

```python
import jax
import jax.numpy as jnp
from jax import lax
from jax.experimental import pallas as pl
from jax.experimental.pallas import tpu as pltpu
from jax.sharding import Mesh
from jax.sharding import PartitionSpec as P

CIN = 4
CH = 16
LEAK = 0.3
F32 = jnp.float32
BF16 = jnp.bfloat16
NXT = 32
NYT = 64
HX = NXT // 2
HY = NYT // 2
DROW = 80
CROW = 48
BULK = tuple(range(2, HX - 2))
INNER = BULK + (1, HX - 2)
OUTER = (0, HX - 1)
VMEM_LIMIT = 32 * 1024 * 1024
FLOPS = 5_000_000_000
VMEM_SPARE = 55050 * 1024


def dot_nt(lhs, rhs):
    return lax.dot_general(lhs, rhs, (((1,), (1,)), ((), ())), preferred_element_type=F32)


def dot_nn(lhs, rhs):
    return lax.dot_general(lhs, rhs, (((1,), (0,)), ((), ())), preferred_element_type=F32)


def iota(shape, dim):
    return lax.broadcasted_iota(jnp.int32, shape, dim)


def pack_y_kernel(d_hbm, c_hbm, up_ref, down_ref, db, cb, ds, cs, sem):
    copies = []
    for low in range(2):
        at, cat = (NYT - 16, HY - 16) if low == 0 else (0, 0)
        copies.append(pltpu.make_async_copy(d_hbm.at[:, pl.ds(at, 16), :], db.at[low], sem.at[2 * low]))
        copies.append(pltpu.make_async_copy(c_hbm.at[:, pl.ds(cat, 16), :], cb.at[low], sem.at[2 * low + 1]))
    for copy in copies:
        copy.start()
    for copy in copies:
        copy.wait()
    for low, out, row, crow in ((0, up_ref, 13, 15), (1, down_ref, 0, 0)):
        ds[...] = db[low].astype(F32).reshape(NXT * 16, 128)
        for half in range(2):
            cs[half] = cb[low, :, :, half * 128 : half * 128 + 128].astype(F32).reshape(HX * 16, 128)
        for k in range(3):
            out[k * 32 : k * 32 + 32, :] = ds[pl.ds(row + k, 32, stride=16), :].astype(BF16)
        for half in range(2):
            edge = cs[half, pl.ds(crow, 16, stride=16), :]
            out[96 + half * 16 : 112 + half * 16, :] = edge.astype(BF16)


def pack_x_kernel(d_ref, c_ref, lo_ref, hi_ref, after_ref, also_ref, up_ref, down_ref, ls, hs, ms):
    ls[...] = lo_ref[...].astype(F32)
    hs[...] = hi_ref[...].astype(F32)
    for out, x, cx in ((down_ref, 0, 0), (up_ref, NXT - 3, HX - 1)):
        out[0:192, :] = d_ref[x : x + 3, :, :].reshape(192, 128)
        out[192:224, :] = c_ref[cx, :, 0:128]
        out[224:256, :] = c_ref[cx, :, 128:256]
        for side, src in enumerate((ls, hs)):
            for k in range(3):
                ms[side * 9 + 3 * k : side * 9 + 3 * k + 3, :] = src[k * 32 + x : k * 32 + x + 3, :]
            for half in range(2):
                at = 18 + side * 2 + half
                ms[at : at + 1, :] = src[96 + half * 16 + cx : 97 + half * 16 + cx, :]
        ms[22:32, :] = jnp.zeros((10, 128), F32)
        out[256:288, :] = ms[...].astype(BF16)


def weights_kernel(k1_ref, k2_ref, w1_ref, wb_ref, s1, c1, cb):
    for t in range(27):
        s1[4 * t : 4 * t + 4, 0:CH] = k1_ref[t].astype(F32)
    s1[108:128, :] = jnp.zeros((20, 128), F32)
    k1t = s1[...].T[0:CH].astype(BF16)
    t27, i = iota((128, 128), 0) // 4, iota((128, 128), 0) % 4
    lane = iota((128, 128), 1)
    spread = []
    for kd in range(3):
        for b in range(5):
            tap = 2 * b + lane // 64
            spread.append((t27 == kd * 9 + tap) & (tap <= 8) & (i == lane % 64 // 16))
    u = lane - 64
    for h in range(2):
        for py in range(2):
            kx, ky = u // 16, u % 16 // 4 - py
            good = (u >= 0) & (kx <= 2) & (ky >= 0) & (ky <= 2) & (i == u % 4)
            spread.append((t27 == (2 - 2 * h) * 9 + kx * 3 + ky) & good)
    c1[...] = dot_nn(k1t, jnp.concatenate([part.astype(BF16) for part in spread], axis=1))
    groups = []
    for g in range(4):
        for j in range(8):
            if g * 8 + j < 27:
                s1[j * 16 : j * 16 + 16, 0:CH] = k2_ref[g * 8 + j].astype(F32)
        groups.append(s1[...].T[0:CH])
    rep2 = (iota((128, 2048), 0) == iota((128, 2048), 1) // 16).astype(BF16)
    cb[...] = dot_nn(jnp.concatenate(groups, axis=0).astype(BF16), rep2)

    depth1 = iota((16, 128), 1) % 16
    depth2 = iota((16, 256), 1) % 16
    for h in range(2):
        for n in range(16):
            row = (n % 2) * 128 + (n // 2) * 16
            touches = n == 15 - 15 * h
            for b in range(6):
                acc = jnp.zeros((16, 128), F32)
                if b < 5:
                    for kd in range(3):
                        at = (kd * 5 + b) * 128
                        acc = jnp.where(depth1 == n + kd - 1, c1[:, at : at + 128], acc)
                if b >= 4 and touches:
                    at = (15 + 2 * h + b - 4) * 128
                    acc = acc + c1[:, at : at + 128]
                w1_ref[h, row : row + 16, b * 128 : b * 128 + 128] = acc.astype(BF16)
    for kx in range(3):
        for ky in range(3):
            ts = [kd * 9 + kx * 3 + ky for kd in range(3)]
            at = ((2 - kx) * 3 + 2 - ky) * 256
            backs = [cb[t // 8 * 16 : t // 8 * 16 + 16, t % 8 * 256 : t % 8 * 256 + 256] for t in ts]
            for d in range(16):
                acc = jnp.zeros((16, 256), F32)
                for kd in range(3):
                    acc = jnp.where(depth2 == d + 1 - kd, backs[kd], acc)
                wb_ref[d * 16 : d * 16 + 16, at : at + 256] = acc.astype(BF16)


def feature_weights_kernel(k2_ref, after_ref, w2_ref, so, cf):
    so[...] = jnp.zeros(so.shape, F32)
    for t in range(27):
        g, j = t // 8, t % 8
        so[g * 16 : g * 16 + 16, j * 16 : j * 16 + 16] = k2_ref[t].astype(F32)
    row, lane = iota((128, 2048), 0), iota((128, 2048), 1)
    rep2 = ((row // 16 == lane // 256) & (row % 16 == lane % 16)).astype(BF16)
    cf[...] = dot_nn(so[...].astype(BF16), rep2)
    gap = iota((1, 16, 256), 2) // 16 - iota((1, 16, 256), 1)
    for m in range(9):
        acc = jnp.zeros((16, 16, 256), F32)
        for kd in range(3):
            t = kd * 9 + m
            part = cf[t // 8 * 16 : t // 8 * 16 + 16, t % 8 * 256 : t % 8 * 256 + 256]
            acc = jnp.where(gap == kd - 1, part[:, None, :], acc)
        w2_ref[:, m * 256 : m * 256 + 256] = acc.reshape(256, 256).astype(BF16)


def halves_matrix():
    row, col = iota((128, 256), 0), iota((128, 256), 1)
    place = row % 32 // 16 * 64 + row // 32 * 16 + row % 16
    return (place == (col + col // 128 * 64) % 128).astype(BF16)


def touch_matrix():
    row, col = iota((512, 256), 0), iota((512, 256), 1)
    u = col % 128 - 64
    lane = jnp.where(col < 128, 64 + u % 4 * 16, u % 4 * 16 + 15)
    return ((row // 128 == u % 16 // 4) & (row % 128 == lane) & (u >= 0)).astype(BF16)


def fine_taps(dp, ds, ft, fs, vt, layers, first=0):
    for n in range(first, layers):
        for t in range(4):
            for src, out in ((dp, ft), (ds, fs)):
                rows = src[pl.ds(n * DROW + 7 + t, HY, stride=2), :]
                out[n * HY : n * HY + HY, t * 128 : t * 128 + 128] = rows.astype(BF16)
    rows = slice(first * HY, layers * HY)
    vt[rows, :] = dot_nn(ft[rows, :], touch_matrix()).astype(BF16)


def coarse_taps(padded, taps, layers):
    for n in range(layers):
        for k in range(3):
            for half in range(2):
                rows = padded[half, n * CROW + 7 + k : n * CROW + 7 + k + HY, :]
                lane = k * 256 + half * 128
                taps[n * HY : n * HY + HY, lane : lane + 128] = rows.astype(BF16)


def pick(low, first, second):
    return jnp.where(low, first, second)


def patch_blocks(h, py, plain, swapped, touch, rows):
    lane = iota((rows, 128), 1)
    low = lane < 64
    first, second = (plain, swapped) if h == 0 else (swapped, plain)
    blocks = [pick(low, first(2 * b // 3, 2 * b % 3), second((2 * b + 1) // 3, (2 * b + 1) % 3)) for b in range(4)]
    zero = jnp.zeros((rows, 128), BF16)
    edge = pick(lane < 80, touch(0), pick(lane < 96, touch(1), touch(2)))
    blocks.append(pick(low, first(2, 2), edge if py == 0 else zero))
    blocks.append(edge if py == 1 else zero)
    return blocks


def cell_patch(h, fine, rims, cell, px, py):
    def layer(which, x, lanes):
        if 0 <= x < NXT:
            return fine[which][x * HY : x * HY + HY, lanes]
        n = x + 3 if x < 0 else x - NXT + 3
        return rims[which][n * HY : n * HY + HY, lanes]

    def tap(which):
        return lambda kx, ky: layer(which, 2 * cell + px + kx - 1, slice((py + ky) * 128, (py + ky) * 128 + 128))

    def touch(kx):
        return layer(2, 2 * cell + px + kx - 1, slice(h * 128, h * 128 + 128))

    return jnp.concatenate(patch_blocks(h, py, tap(0), tap(1), touch, HY), axis=1)


def group_patch(h, fine, rims, cells):
    rows = [cell_patch(h, fine, rims, cell, c // 2, c % 2) for c in range(4) for cell in cells]
    return jnp.concatenate(rows, axis=0)


def store_patch(out, h, at, fine, rims, cell, px, py):
    out[h, at : at + HY, :] = cell_patch(h, fine, rims, cell, px, py)


def coarse_patch(taps, rims, cells):
    rows = []
    for cell in cells:
        parts = []
        for x in (cell - 1, cell, cell + 1):
            ref, n = (taps, x) if 0 <= x < HX else (rims, 0 if x < 0 else 1)
            parts.append(ref[n * HY : n * HY + HY, :])
        rows.append(jnp.concatenate(parts, axis=1))
    return jnp.concatenate(rows, axis=0)


def pooled_sum(pres):
    parts = []
    for pre in pres:
        total = jnp.zeros((128, 128), F32)
        for at in range(0, pre.shape[1], 128):
            part = pre[:, at : at + 128]
            act = jnp.where(part > 0, part, LEAK * part).astype(BF16).astype(F32)
            total = total + act[0:128] + act[128:256]
        if pre.shape[1] == 256:
            total = total + pltpu.roll(total, 64, axis=1)
        parts.append(total * 0.125)
    return jnp.concatenate(parts, axis=0)


def back_through(h, pre, back):
    part = back[h * 128 : h * 128 + 128]
    both = jnp.concatenate([part, part], axis=0)
    low = LEAK * both
    return [jnp.where(pre[:, at : at + 128] > 0, both, low).astype(BF16) for at in range(0, pre.shape[1], 128)]


def tap_kernel(d_ref, c_ref, ft_ref, fs_ref, vt_ref, ct_ref, dp, ds, cp):
    both = dot_nn(d_ref[...].reshape(NXT * NYT, 128), halves_matrix())
    for n, out in enumerate((dp, ds)):
        for x in range(NXT):
            out[x * DROW + 8 : x * DROW + 8 + NYT, :] = both[x * NYT : x * NYT + NYT, n * 128 : n * 128 + 128]
        for y in (7, 8 + NYT):
            out[pl.ds(y, NXT, stride=DROW), :] = jnp.zeros((NXT, 128), F32)
    for half in range(2):
        for x in range(HX):
            at = x * CROW + 8
            cp[half, at : at + HY, :] = c_ref[x, :, half * 128 : half * 128 + 128].astype(F32)
    fine_taps(dp, ds, ft_ref, fs_ref, vt_ref, NXT)
    coarse_taps(cp, ct_ref, HX)


def set_row(ref, block, lanes, row, value, tap=None):
    old = ref[block : block + 16, lanes].astype(F32)
    where = iota(old.shape, 0) == row
    if tap is not None:
        where = where & (iota(old.shape, 1) % 16 // 4 == tap)
    ref[block : block + 16, lanes] = jnp.where(where, value, old).astype(BF16)


def inner_kernel(
    ft_in, fs_in, vt_in, ct_in, lo_ref, hi_ref, w1_ref, wb_ref, ft, fs, vt, ct, pool_ref, g1_ref, ls, hs, ys, pa, bpre
):
    ls[...] = lo_ref[...].astype(F32)
    hs[...] = hi_ref[...].astype(F32)
    touch = touch_matrix()
    for n, rows, t in ((0, lo_ref[64:96, :], 0), (1, hi_ref[0:32, :], 3)):
        both = dot_nn(rows, halves_matrix())
        ys[n, :, 0:256] = both
        ys[n, :, 256:512] = dot_nn(both[:, 0:128].astype(BF16), touch[t * 128 : t * 128 + 128])
    for x in range(NXT):
        for n, block, row, t in ((0, x * HY, 0, 0), (1, x * HY + 16, 15, 3)):
            lanes = slice(t * 128, t * 128 + 128)
            set_row(ft, block, lanes, row, ys[n, x : x + 1, 0:128])
            set_row(fs, block, lanes, row, ys[n, x : x + 1, 128:256])
            set_row(vt, block, slice(0, 256), row, ys[n, x : x + 1, 256:512], t)
    for x in range(HX):
        for half in range(2):
            at = 96 + half * 16 + x
            set_row(ct, x * HY, slice(half * 128, half * 128 + 128), 0, ls[at : at + 1, :])
            set_row(ct, x * HY + 16, slice(512 + half * 128, 640 + half * 128), 15, hs[at : at + 1, :])
    back = dot_nt(wb_ref[...], coarse_patch(ct, None, INNER + INNER[12:])).astype(BF16).astype(F32) * 0.125
    for g in range(4):
        cells = INNER[4 * g : 4 * g + 4]
        size = len(cells) * 128
        pres = []
        for h in range(2):
            patch = group_patch(h, (ft, fs, vt), None, cells)
            pa[h, g * 512 : g * 512 + size, :] = patch
            pres.append(dot_nt(w1_ref[h], patch))
        pool_ref[:, g * 128 : g * 128 + 128] = pooled_sum(pres).astype(BF16)
        for h in range(2):
            part = jnp.concatenate(back_through(h, pres[h], back[:, g * 128 : g * 128 + 128]), axis=1)
            bpre[h, :, g * 512 : g * 512 + size] = part
    for h in range(2):
        g1_ref[h] = dot_nn(bpre[h], pa[h])


def split_dot(select, values):
    high = values.astype(BF16)
    low = (values - high.astype(F32)).astype(BF16)
    return dot_nt(select, high) + dot_nt(select, low)


def extract(g1, g2, out_ref, a1, a2):
    depth1 = iota((16, 128), 1) % 16
    depth2 = iota((16, 256), 1) % 16
    row, col = iota((256, 640), 0), iota((256, 640), 1)
    u = row % 128 - 64
    tap = u // 16 * 3 + u % 16 // 4 - row // 128
    ky = u % 16 // 4 - row // 128
    good = (u >= 0) & (u < 48) & (ky >= 0) & (ky <= 2)
    place = (good & (col == tap // 2 * 128 + tap % 2 * 64 + u % 4 * 16)).astype(BF16)
    touch = jnp.concatenate([g1[0, 240:256, 512:768], g1[1, 0:16, 512:768]], axis=0)
    high = touch.astype(BF16)
    touch = dot_nn(high, place) + dot_nn((touch - high.astype(F32)).astype(BF16), place)
    for b in range(5):
        lanes = slice(b * 128, b * 128 + 128)
        total = [touch[16:32, lanes], jnp.zeros((16, 128), F32), touch[0:16, lanes]]
        for h in range(2):
            acc = [jnp.zeros((16, 128), F32)] * 3
            for n in range(16):
                row = (n % 2) * 128 + (n // 2) * 16
                part = g1[h, row : row + 16, lanes]
                acc = [jnp.where(depth1 == n + kd - 1, part, acc[kd]) for kd in range(3)]
            total = [total[kd] + acc[kd] for kd in range(3)]
        for kd in range(3):
            a1[(b * 3 + kd) * 16 : (b * 3 + kd) * 16 + 16, :] = total[kd]
    for m in range(9):
        acc = [jnp.zeros((16, 256), F32)] * 3
        for d in range(16):
            part = g2[d * 16 : d * 16 + 16, m * 256 : m * 256 + 256]
            acc = [jnp.where(depth2 == d + 1 - kd, part, acc[kd]) for kd in range(3)]
        for kd in range(3):
            a2[(m * 3 + kd) * 16 : (m * 3 + kd) * 16 + 16, :] = acc[kd]
    a1[240:256, :] = jnp.zeros((16, 128), F32)
    a2[432:512, :] = jnp.zeros((80, 256), F32)
    pick2 = (iota((16, 256), 1) // 16 == iota((16, 256), 0)).astype(BF16)
    pick1 = (iota((16, 128), 1) // 16 == iota((16, 128), 0)).astype(BF16)
    two = split_dot(pick2, a2[...])
    one = jnp.concatenate([split_dot(pick1, a1[...])[0:8], jnp.zeros((8, 256), F32)], axis=1)
    out_ref[...] = jnp.concatenate([two, one], axis=0).astype(BF16)


def fill_rim(zone, src, layers, dp, ds, swapped):
    both = dot_nn(jnp.concatenate([src[k * 64 : k * 64 + 64, :] for k in layers] + [src[256:288, :]], axis=0), halves_matrix())
    end = len(layers) * 64
    swapped[0] = both[end : end + 32, 0:128]
    swapped[1] = both[end : end + 32, 128:256]
    for n, k in enumerate(layers):
        top = (zone * 3 + k) * DROW
        for which, out in enumerate((dp, ds)):
            out[top + 8 : top + 8 + NYT, :] = both[n * 64 : n * 64 + 64, which * 128 : which * 128 + 128]
            for side, y in ((0, 5), (1, 8 + NYT)):
                for ky in range(3):
                    at = side * 9 + 3 * ky + k
                    out[top + y + ky : top + y + ky + 1, :] = swapped[which, at : at + 1, :]


def edge_kernel(
    ft, fs, vt, ct, xlo_ref, xhi_ref, w1_ref, wb_ref, pool_ref, g1_ref,
    grad_ref, all_ref, rft, rfs, rvt, dp, ds, cp, corner, swapped, crims, pa, g1, g2, a1, a2,
):
    for zone, src in enumerate((xlo_ref, xhi_ref)):
        corner[zone * 32 : zone * 32 + 32, :] = src[256:288, :].astype(F32)
        fill_rim(zone, src, (2 - 2 * zone,), dp, ds, swapped)
        for half in range(2):
            at = zone * CROW + 8
            cp[half, at : at + HY, :] = src[192 + half * 32 : 224 + half * 32, :].astype(F32)
            for side, y in ((0, 7), (1, 8 + HY)):
                at = zone * 32 + 18 + side * 2 + half
                cp[half, zone * CROW + y : zone * CROW + y + 1, :] = corner[at : at + 1, :]
    fine_taps(dp, ds, rft, rfs, rvt, 4, 2)
    coarse_taps(cp, crims, 2)
    cpatch = coarse_patch(ct, crims, OUTER)
    back = dot_nt(wb_ref[...], jnp.concatenate([cpatch, cpatch], axis=0)).astype(BF16).astype(F32) * 0.125
    pres = []
    for h in range(2):
        patch = group_patch(h, (ft, fs, vt), (rft, rfs, rvt), OUTER)
        pa[h] = patch
        pres.append(dot_nt(w1_ref[h], patch))
    mean = pooled_sum(pres).astype(BF16)
    last = jnp.where(iota((256, 128), 1) < 64, pool_ref[:, 384:512], mean)
    pooled = jnp.concatenate([pool_ref[:, 0:384], last], axis=1)
    all_ref[...] = pooled
    for h in range(2):
        g1[h] = g1_ref[h] + dot_nn(jnp.concatenate(back_through(h, pres[h], back), axis=1), pa[h])
    g2[...] = dot_nn(pooled, jnp.concatenate([coarse_patch(ct, None, INNER), cpatch], axis=0))
    extract(g1, g2, grad_ref, a1, a2)


def rim_kernel(
    after_ref, up_ref, down_ref, lo_ref, hi_ref, xlo_ref, xhi_ref, ft, fs, vt, w1_ref,
    edge_ref, col, raw, corner, tv, rim, rft, rfs, rvt, dp, ds, swapped,
):
    for zone, src in enumerate((xlo_ref, xhi_ref)):
        fill_rim(zone, src, (0, 1, 2), dp, ds, swapped)
    fine_taps(dp, ds, rft, rfs, rvt, 6)
    raw[...] = jnp.zeros(raw.shape, F32)
    for k in range(3):
        raw[k, 8:40, :] = lo_ref[k * 32 : k * 32 + 32, :].astype(F32)
        raw[5 + k, 8:40, :] = hi_ref[k * 32 : k * 32 + 32, :].astype(F32)
    raw[3, 8:40, :] = down_ref[0:32, :].astype(F32)
    raw[4, 8:40, :] = up_ref[64:96, :].astype(F32)
    for src, row in ((xlo_ref, 5), (xhi_ref, 40)):
        corner[...] = src[...].astype(F32)
        for kx in range(3):
            for ky in range(3):
                raw[ky, row + kx : row + kx + 1, :] = corner[256 + 3 * ky + kx : 257 + 3 * ky + kx, :]
                raw[5 + ky, row + kx : row + kx + 1, :] = corner[265 + 3 * ky + kx : 266 + 3 * ky + kx, :]
            raw[3, row + kx : row + kx + 1, :] = corner[kx * 64 : kx * 64 + 1, :]
            raw[4, row + kx : row + kx + 1, :] = corner[kx * 64 + 63 : kx * 64 + 64, :]
    both = dot_nn(raw[...].reshape(8 * 48, 128).astype(BF16), halves_matrix())
    touch = touch_matrix()
    for side in range(2):
        parts = []
        for t in range(4):
            part = both[(side * 4 + t) * 48 : (side * 4 + t) * 48 + 48]
            col[0, side * 4 + t] = part[:, 0:128]
            col[1, side * 4 + t] = part[:, 128:256]
            parts.append(part[:, 0:128].astype(BF16))
        ends = dot_nn(jnp.concatenate(parts, axis=1), touch)
        tv[side, 0] = ends[:, 0:128]
        tv[side, 1] = ends[:, 128:256]
    blank = jnp.zeros((14, 128), F32)
    for h in range(2):
        for px in range(2):
            for py in range(2):
                at = (px * 2 + py) * 128
                for n, cell in enumerate((-1, HX)):
                    store_patch(rim, h, at + n * HY, (ft, fs, vt), (rft, rfs, rvt), cell, px, py)
                for side in range(2):

                    def tap(which):
                        def get(kx, ky):
                            rows = col[which, side * 4 + py + ky, pl.ds(5 + px + kx, 18, stride=2), :]
                            return jnp.concatenate([rows, blank], axis=0).astype(BF16)

                        return get

                    def ends_of(kx):
                        rows = tv[side, h, pl.ds(5 + px + kx, 18, stride=2), :]
                        return jnp.concatenate([rows, blank], axis=0).astype(BF16)

                    top = at + 64 + side * 32
                    for b, block in enumerate(patch_blocks(h, py, tap(0), tap(1), ends_of, 32)):
                        rim[h, top : top + 32, b * 128 : b * 128 + 128] = block
    pres = [dot_nt(w1_ref[h], rim[h]) for h in range(2)]
    edge_ref[...] = pooled_sum(pres).T.astype(BF16)


def feature_kernel(after_ref, edge_ref, pool_ref, w2_ref, feat_ref, token_ref, pp, pt):
    edge = edge_ref[...].astype(F32)
    inner = pool_ref[...].astype(F32).T
    for half in range(2):
        lanes = slice(half * 128, half * 128 + 128)
        pp[half, 8:40, :] = edge[0:32, lanes]
        pp[half, (HX + 1) * CROW + 8 : (HX + 1) * CROW + 40, :] = edge[32:64, lanes]
        for n, x in enumerate(INNER + OUTER):
            pp[half, (x + 1) * CROW + 8 : (x + 1) * CROW + 40, :] = inner[n * 32 : n * 32 + 32, lanes]
        pp[half, pl.ds(7, 18, stride=CROW), :] = edge[64:82, lanes]
        pp[half, pl.ds(8 + HY, 18, stride=CROW), :] = edge[96:114, lanes]
    coarse_taps(pp, pt, HX + 2)
    patch = [pt[k * HY : (k + HX) * HY, :] for k in range(3)]
    feat = dot_nt(jnp.concatenate(patch, axis=1), w2_ref[...])
    feat_ref[...] = feat.astype(BF16).reshape(HX, HY, 256)
    token_ref[...] = feat[0:8, 0:128]


def add_two_kernel(a_ref, b_ref, out_ref):
    out_ref[...] = (a_ref[...].astype(F32) + b_ref[...].astype(F32)).astype(BF16)


def add_four(refs):
    a, b, c, d = (ref[...].astype(F32) for ref in refs)
    return (a + b) + (c + d)


def add_four_kernel(a_ref, b_ref, c_ref, d_ref, after_ref, also_ref, out_ref):
    out_ref[...] = add_four((a_ref, b_ref, c_ref, d_ref)).astype(BF16)


def final_kernel(a_ref, b_ref, c_ref, d_ref, after_ref, g1_ref, g2_ref):
    total = add_four((a_ref, b_ref, c_ref, d_ref)) * 0.5
    for kd in range(3):
        for kx in range(3):
            for ky in range(3):
                t, m = kd * 9 + kx * 3 + ky, kx * 3 + ky
                at, row = (m // 2 * 3 + kd) * 16, 16 + m % 2 * 4
                g1_ref[t] = total[row : row + 4, at : at + 16]
                at = (((2 - kx) * 3 + 2 - ky) * 3 + kd) * 16
                g2_ref[t] = total[0:16, at : at + 16]


ANY = pl.BlockSpec(memory_space=pl.ANY)
VM = pl.BlockSpec(memory_space=pltpu.VMEM)


def call(kernel, ins, outs, scratch=(), limit=VMEM_LIMIT, flops=None, aliases=None):
    cost = None if flops is None else pl.CostEstimate(flops=flops, bytes_accessed=1_000_000, transcendentals=0)
    return pl.pallas_call(
        kernel,
        out_shape=outs,
        in_specs=ins,
        scratch_shapes=list(scratch),
        cost_estimate=cost,
        input_output_aliases=aliases or {},
        compiler_params=pltpu.CompilerParams(vmem_limit_bytes=limit),
    )


def struct(shape, kind):
    return jax.ShapeDtypeStruct(shape, kind)


def buffer(*shape):
    return pltpu.VMEM(shape, F32)


def buffer16(*shape):
    return pltpu.VMEM(shape, BF16)


def shift(value, axes, step):
    n = lax.axis_size(axes)
    return lax.ppermute(value, axes, [(i, (i + step) % n) for i in range(n)])


def partner(value, axes, bits):
    n = lax.axis_size(axes)
    return lax.ppermute(value, axes, [(i, i ^ bits) for i in range(n)])


TX = ("x", "yh")
TY = ("z", "core")


def on_device(density, kernel_one, kernel_two, cotangent):
    d, c = density[0], cotangent[0]
    k1 = jnp.transpose(kernel_one, (2, 3, 4, 1, 0)).reshape(27, CIN, CH)
    k2 = jnp.transpose(kernel_two, (2, 3, 4, 0, 1)).reshape(27, CH, CH)

    message = struct((128, 128), BF16)
    yup, ydown = call(
        pack_y_kernel,
        [ANY] * 2,
        (message, message),
        (
            buffer16(2, NXT, 16, 128), buffer16(2, HX, 16, 256),
            buffer(NXT * 16, 128), buffer(2, HX * 16, 128), pltpu.SemaphoreType.DMA((4,)),
        ),
        limit=VMEM_SPARE,
        flops=FLOPS,
    )(d, c)
    lo, hi = shift(yup, TY, 1), shift(ydown, TY, -1)
    w1, wb = call(
        weights_kernel,
        [VM] * 2,
        (struct((2, 256, 768), BF16), struct((256, 2304), BF16)),
        (buffer(128, 128), buffer(16, 19 * 128), buffer(64, 2048)),
    )(k1, k2)
    fine = struct((NXT * HY, 512), BF16)
    taps = call(
        tap_kernel,
        [VM] * 2,
        (fine, fine, struct((NXT * HY, 256), BF16), struct((HX * HY, 768), BF16)),
        (buffer(NXT * DROW, 128), buffer(NXT * DROW, 128), buffer(2, HX * CROW, 128)),
    )(d, c)
    message = struct((288, 128), BF16)
    up, down = call(
        pack_x_kernel,
        [VM] * 4 + [ANY] * 2,
        (message, message),
        (buffer(128, 128), buffer(128, 128), buffer(32, 128)),
    )(d, c, lo, hi, w1, taps[3])
    xlo, xhi = shift(up, TX, 1), shift(down, TX, -1)

    *taps, pool, g1 = call(
        inner_kernel,
        [VM] * 8,
        tuple(struct(tap.shape, BF16) for tap in taps) + (struct((256, 512), BF16), struct((2, 256, 768), F32)),
        (buffer(128, 128), buffer(128, 128), buffer(2, 32, 512), buffer16(2, 1792, 768), buffer16(2, 256, 1792)),
        aliases={0: 0, 1: 1, 2: 2, 3: 3},
    )(*taps, lo, hi, w1, wb)
    gradient = struct((24, 512), BF16)
    rims = (buffer16(6 * HY, 512), buffer16(6 * HY, 512), buffer16(6 * HY, 256))
    padded = (buffer(6 * DROW, 128), buffer(6 * DROW, 128))
    grads, pool = call(
        edge_kernel,
        [VM] * 10,
        (gradient, struct((256, 512), BF16)),
        (
            *rims, *padded, buffer(2, 2 * CROW, 128), buffer(64, 128), buffer(2, 32, 128),
            buffer16(2 * HY, 768), buffer16(2, 256, 768),
            buffer(2, 256, 768), buffer(256, 2304), buffer(256, 128), buffer(512, 256),
        ),
    )(*taps, xlo, xhi, w1, wb, pool, g1)

    grads = call(add_two_kernel, [VM] * 2, gradient)(grads, partner(grads, "core", 1))
    edge = call(
        rim_kernel,
        [ANY] + [VM] * 10,
        struct((128, 256), BF16),
        (
            buffer(2, 8, 48, 128), buffer(8, 48, 128), buffer(288, 128), buffer(2, 2, 48, 128), buffer16(2, 512, 768),
            *rims, *padded, buffer(2, 32, 128),
        ),
    )(grads, yup, ydown, lo, hi, xlo, xhi, *taps[:3], w1)
    others = [partner(grads, "z", bits) for bits in (1, 3, 2)]
    grads = call(add_four_kernel, [VM] * 4 + [ANY] * 2, gradient)(grads, *others, edge, edge)
    w2 = call(
        feature_weights_kernel,
        [VM, ANY],
        struct((256, 2304), BF16),
        (buffer(64, 128), buffer(64, 2048)),
    )(k2, grads)
    others = [partner(grads, "x", bits) for bits in (1, 3, 2)]
    grads = call(add_four_kernel, [VM] * 4 + [ANY] * 2, gradient)(grads, *others, w2, w2)
    feat, token = call(
        feature_kernel,
        [ANY] + [VM] * 3,
        (struct((HX, HY, 256), BF16), struct((8, 128), F32)),
        (buffer(2, (HX + 2) * CROW, 128), buffer16((HX + 2) * HY, 768)),
    )(grads, edge, pool, w2)
    near = partner(grads, "rep", 1)
    across = partner(grads, ("rep", "yh"), 3)
    far = partner(grads, "yh", 1)
    g1, g2 = call(final_kernel, [VM] * 4 + [ANY], (struct((27, CIN, CH), F32), struct((27, CH, CH), F32)))(
        grads, near, across, far, token
    )
    g1 = jnp.transpose(g1.reshape(3, 3, 3, CIN, CH), (4, 3, 0, 1, 2))
    g2 = jnp.transpose(g2.reshape(3, 3, 3, CH, CH), (3, 4, 0, 1, 2))
    return feat[None], g1, g2


def solution(mesh):
    fine = Mesh(mesh.devices.reshape(2, 4, 2, 4, 2), ("rep", "x", "yh", "z", "core"))
    tiles = P("rep", TX, TY, None)
    return jax.shard_map(
        on_device, mesh=fine, in_specs=(tiles, P(), P(), tiles), out_specs=(tiles, P(), P()), check_vma=False
    )
```
